256 devices in a mesh: section: 8 (over z_hi, core), dp: 32 (over y, x, z_lo).
Axes of the slice: x: 4, y: 4, z: 8 (z_hi: 4, z_lo: 2; z = z_hi * 2 + z_lo), core: 2. Of those that a mesh axis runs over, the one named last changes fastest.
Arguments:
- inputs: bfloat16 [4096, 7168], P('dp'), may hold values from -6 to 6
- cotangent: bfloat16 [4096, 7168], P('dp'), may hold values from -6 to 6
- adapt_in: bfloat16 [8, 7168, 128], P('section'), may hold values from -0.0625 to 0.0625
- adapt_out: bfloat16 [8, 7168, 128], P('section'), may hold values from -0.5 to 0.5
- probe_in: bfloat16 [8, 7168, 128], P('section'), may hold values from -0.0625 to 0.0625
- probe_out: bfloat16 [8, 7168, 128], P('section'), may hold values from -0.5 to 0.5
Outputs:
- diag_in: float32 [8, 7168, 128], P('section', 'dp')
- diag_out: float32 [8, 7168, 128], P('section', 'dp')
The draws below stay inside these ranges and needn't reach their ends.
All inputs are finite; a program needn't handle non-finite values.
Results may differ from the reference program's by a relative error of at most 0.027.
Values may be sent and summed in bfloat16 or wider, within the bound.
No kernel may reach another device: no remote copies, remote signals or barrier semaphores. Data moves between devices by JAX's collectives and lax.ppermute only.
A program may use at most 128 MiB of HBM per device.

```python
import jax
import jax.numpy as jnp
from jax import lax

D = 7168
RANK = 128
MB = 16
SECTIONS = 8
TOKENS = 4096
N_SECTION = 8


def with_spikes(values, rng, source, target, parts, factor):
    owner, partner = [(jnp.arange(values.shape[dim]) // (values.shape[dim] // parts)).reshape([-1 if axis == dim else 1 for axis in range(values.ndim)]) for dim in (source, target)]
    chosen = jax.random.permutation(rng, parts)[partner]
    strong = (owner == chosen) | (owner == (partner + parts // 2) % parts)
    return jnp.where(strong, factor * values, values)


def block_scale(own_key, shape, cuts, least, largest):
    factor_of, own = 1.0, jax.random.fold_in(own_key, 6)
    for dim, shards_of in cuts:
        draws = jnp.exp(jax.random.uniform(jax.random.fold_in(own, dim), (shards_of,), jnp.float32, least / len(cuts), largest / len(cuts)))
        factor_of = factor_of * jnp.repeat(draws, shape[dim] // shards_of).reshape([-1 if axis == dim else 1 for axis in range(len(shape))])
    return factor_of


def scatter_about(rng, shape, deviation, bound, split=(), held_as=jnp.bfloat16):
    entries = jax.random.normal(rng, shape, jnp.float32) * deviation
    if len(split) > 0:
        entries = block_scale(rng, shape, split, -0.22, 0.18) * entries
    return jnp.clip(entries, min=-bound, max=bound).astype(held_as)


def noise_with(own_key, shape, width, limit, shards, heavy, held_as=jnp.bfloat16):
    values = width * jax.random.normal(own_key, shape, jnp.float32)
    if shards:
        values = values * block_scale(own_key, shape, shards, -0.22, 0.18)
    return jnp.clip(with_spikes(values, jax.random.fold_in(own_key, 3), *heavy), -limit, limit).astype(held_as)


def setup_inputs(seed: int = 0) -> dict:
    key_list = jax.random.split(jax.random.key(seed), 7)
    inputs = noise_with(key_list[0], (TOKENS, D), 1.0, 6.0, ((0, 32),), (0, 1, 32, 2.75))
    cotangent = scatter_about(key_list[1], (TOKENS, D), 1.0, 6.0, ((0, 32),))
    adapt_in = scatter_about(key_list[2], (SECTIONS, D, RANK), D ** -0.5, 0.0625, ((0, 8),))
    adapt_out = scatter_about(key_list[3], (SECTIONS, D, RANK), RANK ** -0.5, 0.5, ((0, 8),))
    probe_in = scatter_about(key_list[4], (SECTIONS, D, RANK), D ** -0.5, 0.0625, ((0, 8),))
    probe_out = scatter_about(key_list[5], (SECTIONS, D, RANK), RANK ** -0.5, 0.5, ((0, 8),))
    return {"inputs": inputs, "cotangent": cotangent, "adapt_in": adapt_in, "adapt_out": adapt_out, "probe_in": probe_in, "probe_out": probe_out}


eps = 1e-05

def matmul(left, right):
    return jnp.dot(left, right, preferred_element_type=jnp.float32)

def matmul_last(left, right):
    return lax.dot_general(left, right, (((1,), (1,)), ((), ())), preferred_element_type=jnp.float32)

def matmul_rows(left, right):
    return lax.dot_general(left, right, (((0,), (0,)), ((), ())), preferred_element_type=jnp.float32)

def rms_scale(values):
    return values * lax.rsqrt(lax.optimization_barrier(jnp.mean(values * values, axis=-1, keepdims=True)) + eps)

def rms_back(values, grads):
    scale = lax.rsqrt(lax.optimization_barrier(jnp.mean(values * values, axis=-1, keepdims=True)) + eps)
    return scale * grads - values * scale ** 3 * lax.optimization_barrier(jnp.mean(grads * values, axis=-1, keepdims=True))

def activations(primal, tangent, w_in, p_in):
    primal32 = primal.astype(jnp.float32)
    tangent32 = tangent.astype(jnp.float32)
    normed, normed_t = jax.jvp(rms_scale, (primal32,), (tangent32,))
    normed_b = normed.astype(jnp.bfloat16)
    normed_tb = normed_t.astype(jnp.bfloat16)
    pre_act = matmul(normed_b, w_in)
    pre_tan = matmul(normed_tb, w_in) + matmul(normed_b, p_in)
    sigmoid_a = jax.nn.sigmoid(pre_act)
    slope = sigmoid_a * (1.0 + pre_act * (1.0 - sigmoid_a))
    hidden_b = (pre_act * sigmoid_a).astype(jnp.bfloat16)
    hidden_tb = (slope * pre_tan).astype(jnp.bfloat16)
    return (primal32, tangent32, normed_b, normed_tb, pre_act, pre_tan, sigmoid_a, slope, hidden_b, hidden_tb)

def forward_section(primal, tangent, w_in, w_out, p_in, p_out):
    primal32, tangent32, _, _, _, _, _, _, hidden_b, hidden_tb = activations(primal, tangent, w_in, p_in)
    result = primal32 + matmul_last(hidden_b, w_out)
    result_t = tangent32 + matmul_last(hidden_tb, w_out) + matmul_last(hidden_b, p_out)
    return (result.astype(jnp.bfloat16), result_t.astype(jnp.bfloat16))

def backward_section(primal, tangent, adjoint, adj_tangent, w_in, w_out, p_in, p_out):
    primal32, tangent32, normed_b, normed_tb, pre_act, pre_tan, sigmoid_a, slope, hidden_b, hidden_tb = activations(primal, tangent, w_in, p_in)
    bend = sigmoid_a * (1.0 - sigmoid_a) * (2.0 + pre_act * (1.0 - 2.0 * sigmoid_a))
    grad_h = matmul(adjoint, w_out)
    grad_ht = matmul(adj_tangent, w_out) + matmul(adjoint, p_out)
    term_out = matmul_rows(adj_tangent, hidden_b) + matmul_rows(adjoint, hidden_tb)
    grad_pre = (grad_h * slope).astype(jnp.bfloat16)
    grad_pt = (grad_ht * slope + grad_h * bend * pre_tan).astype(jnp.bfloat16)
    term_in = matmul_rows(normed_tb, grad_pre) + matmul_rows(normed_b, grad_pt)
    grad_n = matmul_last(grad_pre, w_in)
    grad_nt = matmul_last(grad_pt, w_in) + matmul_last(grad_pre, p_in)
    back, back_t = jax.jvp(rms_back, (primal32, grad_n), (tangent32, grad_nt))
    grad_x = adjoint.astype(jnp.float32) + back
    grad_xt = adj_tangent.astype(jnp.float32) + back_t
    return (grad_x.astype(jnp.bfloat16), grad_xt.astype(jnp.bfloat16), p_in.astype(jnp.float32) * term_in, p_out.astype(jnp.float32) * term_out)

def reference(inputs, cotangent, adapt_in, adapt_out, probe_in, probe_out):
    count = inputs.shape[0] // MB

    def block(carry, index):
        sum_in, sum_out = carry
        start = (index * MB).astype(jnp.int32)
        primal = lax.dynamic_slice_in_dim(inputs, start, MB, 0)
        tangent = jnp.zeros_like(primal)
        saved = []
        for section in range(N_SECTION):
            saved.append((primal, tangent))
            primal, tangent = forward_section(primal, tangent, adapt_in[section], adapt_out[section], probe_in[section], probe_out[section])
        adjoint = lax.dynamic_slice_in_dim(cotangent, start, MB, 0)
        adj_tangent = jnp.zeros_like(adjoint)
        for section in reversed(range(N_SECTION)):
            adjoint, adj_tangent, term_in, term_out = backward_section(saved[section][0], saved[section][1], adjoint, adj_tangent, adapt_in[section], adapt_out[section], probe_in[section], probe_out[section])
            sum_in = sum_in.at[section].add(term_in)
            sum_out = sum_out.at[section].add(term_out)
        return ((sum_in, sum_out), None)
    empty = jnp.zeros(adapt_in.shape, jnp.float32)
    (sum_in, sum_out), _ = lax.scan(block, (empty, empty), jnp.arange(count, dtype=jnp.int32))
    return (sum_in, sum_out)
```

```python
import functools

import jax
import jax.numpy as jnp
from jax import lax
from jax.experimental import pallas as pl
from jax.experimental.pallas import tpu as pltpu
from jax.sharding import Mesh, PartitionSpec as P

EPS = 1e-05
R = 128
SECTIONS = 8
BLOCKS = 24
SEC = ("zh", "c")
DP = ("y", "x", "zl")
BF = jnp.bfloat16
F32 = jnp.float32


def mm(left, right):
    return jnp.dot(left, right, preferred_element_type=F32)


def mm_nt(left, right):
    return lax.dot_general(left, right, (((1,), (1,)), ((), ())), preferred_element_type=F32)


def mm_tn(left, right):
    return lax.dot_general(left, right, (((0,), (0,)), ((), ())), preferred_element_type=F32)


def call(kernel, **kw):
    return pl.pallas_call(kernel, **kw)


def project_kernel(x_ref, c_ref, a_ref, p_ref, b_ref, q_ref, out_ref, ss_ref, acc, acc_ss):
    step = pl.program_id(0)

    @pl.when(step == 0)
    def _():
        acc[...] = jnp.zeros_like(acc)
        acc_ss[...] = jnp.zeros_like(acc_ss)

    x = x_ref[...]
    rows = x.shape[0]
    x32 = x.astype(F32)
    acc_ss[...] += jnp.sum(x32 * x32, axis=-1, keepdims=True)
    ap = jnp.concatenate([a_ref[0], p_ref[0]], axis=1)
    bq = jnp.concatenate([b_ref[0], q_ref[0]], axis=1)
    acc[:, : 2 * R] += mm(x, ap)
    both = mm(jnp.concatenate([x, c_ref[...]], axis=0), bq)
    acc[:, 2 * R : 4 * R] += both[:rows]
    acc[:, 4 * R :] += both[rows:]

    @pl.when(step == pl.num_programs(0) - 1)
    def _():
        out_ref[...] = acc[...].astype(BF)
        ss_ref[...] = acc_ss[...]


def project(x, c, a, p, b, q):
    rows, width = x.shape
    block = width // 7
    wide = pl.BlockSpec((rows, block), lambda k: (0, k))
    weight = pl.BlockSpec((1, block, R), lambda k: (0, k, 0))
    return call(
        project_kernel,
        grid=(7,),
        in_specs=[wide, wide, weight, weight, weight, weight],
        out_specs=[
            pl.BlockSpec((rows, 6 * R), lambda k: (0, 0)),
            pl.BlockSpec((rows, R), lambda k: (0, 0)),
        ],
        out_shape=[
            jax.ShapeDtypeStruct((rows, 6 * R), BF),
            jax.ShapeDtypeStruct((rows, R), F32),
        ],
        scratch_shapes=[pltpu.VMEM((rows, 6 * R), F32), pltpu.VMEM((rows, R), F32)],
        compiler_params=pltpu.CompilerParams(vmem_limit_bytes=32 * 1024 * 1024),
        cost_estimate=pl.CostEstimate(
            flops=2 * rows * width * 6 * R,
            bytes_accessed=4 * rows * width + 8 * width * R,
            transcendentals=0,
        ),
    )(x, c, a, p, b, q)


def gram_kernel(me_ref, w_ref, out_ref):
    me = me_ref[0]

    def cols(section, names):
        return jnp.concatenate([w_ref[section, n] for n in names], axis=1)

    def put(at, block):
        out_ref[at * R : (at + 1) * R] = block.astype(BF)

    for k in range(1, 5):
        other = lax.rem(me + k, SECTIONS)
        low, high = jnp.minimum(me, other), jnp.maximum(me, other)
        right = cols(high, (0, 1, 2, 3))
        from_b = mm_tn(w_ref[low, 2], right)
        from_q = mm_tn(w_ref[low, 3], cols(high, (0, 2)))
        six = [from_b[:, i * R : (i + 1) * R] for i in range(4)]
        six += [from_q[:, i * R : (i + 1) * R] for i in range(2)]
        if k < 4:
            for i in range(6):
                put((k - 1) * 6 + i, six[i])
        else:
            first = me < 4
            for i in range(3):
                put(18 + i, jnp.where(first, six[i], six[3 + i]))
    own = mm_tn(w_ref[me, 2], cols(me, (2, 3)))
    put(21, own[:, :R])
    put(22, own[:, R:])
    put(23, jnp.zeros((R, R), F32))


def gram(me, w_all):
    return call(
        gram_kernel,
        in_specs=[
            pl.BlockSpec(memory_space=pltpu.SMEM),
            pl.BlockSpec(memory_space=pltpu.VMEM),
        ],
        out_specs=pl.BlockSpec(memory_space=pltpu.VMEM),
        out_shape=jax.ShapeDtypeStruct((BLOCKS * R, R), BF),
        compiler_params=pltpu.CompilerParams(vmem_limit_bytes=32 * 1024 * 1024),
        cost_estimate=pl.CostEstimate(
            flops=2 * w_all.shape[2] * BLOCKS * R * R,
            bytes_accessed=w_all.size * 2,
            transcendentals=0,
        ),
    )(me, w_all)


def place(low, high):
    gap = high - low
    if gap <= 3:
        return [(low, (gap - 1) * 6 + i) for i in range(6)]
    if gap == 4:
        return [(low, 18 + i) for i in range(3)] + [(high, 18 + i) for i in range(3)]
    return [(high, (7 - gap) * 6 + i) for i in range(6)]


def relay_kernel(axes, piece, width, pxc_ref, ss_ref, g_hbm, out_ref, g, sem, saved, left, dleft):
    nzh, nc, ny, nx, nzl = axes
    ndp = ny * nx * nzl

    def fetch(index, _):
        zl = lax.rem(index, nzl)
        zh = lax.rem(index // nzl, nzh)
        x = lax.rem(index // (nzl * nzh), nx)
        y = lax.rem(index // (nzl * nzh * nx), ny)
        c = index // (nzl * nzh * nx * ny)
        owner = zh * nc + c
        dp = (y * nx + x) * nzl + zl
        pltpu.make_async_copy(
            g_hbm.at[pl.ds(pl.multiple_of(index * piece, 16), piece)],
            g.at[pl.ds(pl.multiple_of((owner * ndp + dp) * piece, 16), piece)],
            sem,
        ).start()
        return 0

    lax.fori_loop(0, SECTIONS * ndp, fetch, 0)
    pltpu.make_async_copy(g_hbm, g, sem).wait()

    def block(at):
        start = (at[0] * BLOCKS + at[1]) * R
        return g[start : start + R]

    rows = pxc_ref.shape[1]
    ss = ss_ref[...][:, :1]
    st = jnp.zeros_like(ss)
    rsum = lambda v: jnp.sum(v, axis=-1, keepdims=True)
    hs, dhs, scales, mus = [], [], [], []
    for s in range(SECTIONS):
        base = pxc_ref[s][:, : 4 * R].astype(F32)
        prim, tan = base, None
        if s:
            both = None
            from_q = None
            for j in range(s):
                at = place(j, s)
                right = jnp.concatenate([block(at[i]) for i in range(4)], axis=1)
                part = mm(jnp.concatenate([hs[j], dhs[j]], axis=0), right)
                both = part if both is None else both + part
                rq = jnp.concatenate([block(at[4]), block(at[5])], axis=1)
                part = mm(hs[j], rq)
                from_q = part if from_q is None else from_q + part
            prim = base + both[:rows]
            ta = both[rows:, :R] + from_q[:, :R]
            tb = both[rows:, 2 * R : 3 * R] + from_q[:, R:]
        else:
            ta = tb = jnp.zeros((rows, R), F32)
        xa, xp = prim[:, :R], prim[:, R : 2 * R]
        r = lax.rsqrt(ss / width + EPS)
        mu = r * r * r * (st / width)
        pre = r * xa
        dpre = r * (ta + xp) - mu * xa
        sig = 1.0 / (1.0 + jnp.exp(-pre))
        slope = sig * (1.0 + pre * (1.0 - sig))
        bend = sig * (1.0 - sig) * (2.0 + pre * (1.0 - 2.0 * sig))
        h = (pre * sig).astype(BF)
        dh = (slope * dpre).astype(BF)
        hs.append(h)
        dhs.append(dh)
        scales.append(r)
        mus.append(mu)
        own = jnp.concatenate([block((s, 21)), block((s, 22))], axis=1)
        step = mm(h, own)
        xb_new = prim[:, 2 * R : 3 * R] + step[:, :R]
        xq_new = prim[:, 3 * R :] + step[:, R:]
        tb_new = tb + mm(dh, block((s, 21))) + mm_nt(h, block((s, 22)))
        h32, dh32 = h.astype(F32), dh.astype(F32)
        ss = ss + rsum(h32 * (prim[:, 2 * R : 3 * R] + xb_new))
        st = st + rsum(dh32 * xb_new + h32 * (xq_new + tb))
        for i, value in enumerate((xa, ta + xp, xb_new, xq_new, tb_new, slope, bend * dpre)):
            saved[s, i] = value
        out_ref[s, 0] = h
        out_ref[s, 1] = dh

    total = jnp.zeros_like(ss)
    dtotal = jnp.zeros_like(ss)
    for s in reversed(range(SECTIONS)):
        xa, xd, xb_new, xq_new, tb_new, slope, curve = [saved[s, i] for i in range(7)]
        fresh = pxc_ref[s][:, 4 * R :].astype(F32)
        gb = fresh[:, :R] - total * xb_new
        gq = fresh[:, R:] - total * xq_new
        dgb = -(dtotal * xb_new + total * tb_new)
        for i in range(s + 1, SECTIONS):
            at = place(s, i)
            right = jnp.concatenate([block(at[n]) for n in range(4)], axis=1)
            both = mm_nt(jnp.concatenate([left[i], dleft[i]], axis=0), right)
            gb = gb + both[:rows]
            dgb = dgb + both[rows:]
            rq = jnp.concatenate([block(at[4]), block(at[5])], axis=1)
            li = left[i]
            gq = gq + mm_nt(jnp.concatenate([li[:, :R], li[:, 2 * R : 3 * R]], axis=1), rq)
        dgh = dgb + gq
        ga = gb * slope
        dga = dgh * slope + gb * curve
        r, mu = scales[s], mus[s]
        u = (r * dga - mu * ga).astype(BF)
        v = (r * ga).astype(BF)
        h, dh = hs[s], dhs[s]
        h32, dh32 = h.astype(F32), dh.astype(F32)
        z = (-total * h32).astype(BF)
        y = (-(dtotal * h32 + total * dh32)).astype(BF)
        zero = jnp.zeros_like(z)
        left[s] = jnp.concatenate([v, zero, z, zero], axis=1)
        dleft[s] = jnp.concatenate([u, v, y, z], axis=1)
        out_ref[s, 2] = u
        out_ref[s, 3] = v
        out_ref[s, 4] = z
        out_ref[s, 5] = y
        inner = rsum(ga * xa) / width
        dinner = rsum(dga * xa + ga * xd) / width
        total = total + r * r * r * inner
        dtotal = dtotal + r * r * r * dinner - 3.0 * r * r * mu * inner


def relay(axes, width, pxc, ss, g):
    rows = pxc.shape[1]
    piece = g.shape[0] // (axes[0] * axes[1] * axes[2] * axes[3] * axes[4])
    vm = pl.BlockSpec(memory_space=pltpu.VMEM)
    return call(
        functools.partial(relay_kernel, axes, piece, float(width)),
        in_specs=[vm, vm, pl.BlockSpec(memory_space=pl.ANY)],
        out_specs=vm,
        out_shape=jax.ShapeDtypeStruct((SECTIONS, 6, rows, R), BF),
        scratch_shapes=[
            pltpu.VMEM(g.shape, BF),
            pltpu.SemaphoreType.DMA,
            pltpu.VMEM((SECTIONS, 7, rows, R), F32),
            pltpu.VMEM((SECTIONS, rows, 4 * R), BF),
            pltpu.VMEM((SECTIONS, rows, 4 * R), BF),
        ],
        compiler_params=pltpu.CompilerParams(vmem_limit_bytes=48 * 1024 * 1024),
        cost_estimate=pl.CostEstimate(
            flops=2 * 28 * 20 * rows * R * R, bytes_accessed=g.size * 2, transcendentals=0
        ),
    )(pxc, ss, g)


def terms_kernel(me_ref, x_ref, c_ref, own_ref, other_ref, out_ref):
    me = me_ref[0]
    i = pl.program_id(0)
    part = out_ref.shape[0]
    slab = x_ref.shape[1] // part
    h, dh, u, v, z, y = [own_ref[0, n] for n in range(6)]
    hi, dhi, ui, vi, zi, yi = [other_ref[0, n] for n in range(6)]
    from_x = mm_tn(x_ref[...], jnp.concatenate([u, y], axis=1))
    from_c = mm_tn(c_ref[...], dh)
    t_in = from_x[:, :R].astype(BF)
    t_out = (from_x[:, R:] + from_c).astype(BF)
    for n in range(part):
        out_ref[n, :slab] = t_in[n * slab : (n + 1) * slab]
        out_ref[n, slab : 2 * slab] = t_out[n * slab : (n + 1) * slab]

    below = i < me
    upto = i <= me

    def pair(p0, p1, r0, r1):
        wide = mm_tn(p0, jnp.concatenate([r0, r1], axis=1))
        return wide[:, :R] + mm_tn(p1, r1), wide[:, R:]

    m0, m1 = pair(
        jnp.where(below, hi, vi),
        jnp.where(below, dhi, ui),
        jnp.where(below, u, dh),
        jnp.where(below, v, h),
    )
    m2, m3 = pair(
        jnp.where(upto, hi, zi),
        jnp.where(upto, dhi, yi),
        jnp.where(upto, y, dh),
        jnp.where(upto, z, h),
    )
    keep = i != me
    four = [jnp.where(keep, m0, 0.0), jnp.where(keep, m1, 0.0), m2, m3]
    each = 4 // part
    for n in range(part):
        for e in range(each):
            out_ref[n, 2 * slab + e * R : 2 * slab + (e + 1) * R] = four[n * each + e].astype(BF)


def terms(me, ndp, x, c, coef):
    rows, width = x.shape
    part = ndp // SECTIONS
    slab = width // ndp
    high = 2 * slab + 4 // part * R
    block = width // SECTIONS
    wide = pl.BlockSpec((rows, block), lambda i, me: (0, i))
    one = (1, 6, rows, R)
    return call(
        terms_kernel,
        grid_spec=pltpu.PrefetchScalarGridSpec(
            num_scalar_prefetch=1,
            grid=(SECTIONS,),
            in_specs=[
                wide,
                wide,
                pl.BlockSpec(one, lambda i, me: (me[0], 0, 0, 0)),
                pl.BlockSpec(one, lambda i, me: (i, 0, 0, 0)),
            ],
            out_specs=pl.BlockSpec((part, high, R), lambda i, me: (i, 0, 0)),
        ),
        out_shape=jax.ShapeDtypeStruct((ndp, high, R), BF),
        compiler_params=pltpu.CompilerParams(vmem_limit_bytes=32 * 1024 * 1024),
        cost_estimate=pl.CostEstimate(
            flops=2 * rows * width * 3 * R, bytes_accessed=8 * rows * width, transcendentals=0
        ),
    )(me, x, c, coef, coef)


def finish_kernel(me_ref, t_ref, w_ref, m_ref, in_ref, out_ref):
    me = me_ref[0]
    slab = w_ref.shape[2]
    t_in, t_out = t_ref[:slab], t_ref[slab:]
    for i in range(SECTIONS):
        below = i < me
        a, p, b, q = [w_ref[i, n] for n in range(4)]
        first = jnp.concatenate([jnp.where(below, b, a), jnp.where(below, q, p)], axis=1)
        product = mm(first, m_ref[i, : 2 * R])
        t_in = t_in + jnp.where(below, product, 0.0)
        t_out = t_out + jnp.where(below, 0.0, product)
        t_out = t_out + mm(jnp.concatenate([b, q], axis=1), m_ref[i, 2 * R :])
    in_ref[...] = w_ref[me, 1].astype(F32) * t_in
    out_ref[...] = w_ref[me, 3].astype(F32) * t_out


def finish(me, t, w_all, m):
    vm = pl.BlockSpec(memory_space=pltpu.VMEM)
    shape = jax.ShapeDtypeStruct((w_all.shape[2], R), F32)
    return call(
        finish_kernel,
        in_specs=[pl.BlockSpec(memory_space=pltpu.SMEM), vm, vm, vm],
        out_specs=[vm, vm],
        out_shape=[shape, shape],
        compiler_params=pltpu.CompilerParams(vmem_limit_bytes=32 * 1024 * 1024),
    )(me, t, w_all, m)


def on_device(axes, inputs, cotangent, adapt_in, adapt_out, probe_in, probe_out):
    nzh, nc, ny, nx, nzl = axes
    ndp = ny * nx * nzl
    rows, width = inputs.shape
    slab = width // ndp
    me = lax.axis_index(SEC).astype(jnp.int32).reshape(1)
    dp = lax.axis_index(DP)

    own = jnp.stack(
        [
            lax.dynamic_slice_in_dim(w[0], dp * slab, slab, 0)
            for w in (adapt_in, probe_in, adapt_out, probe_out)
        ]
    )
    w_all = lax.all_gather(own, SEC)
    projected, ss = project(inputs, cotangent, adapt_in, probe_in, adapt_out, probe_out)
    pxc = lax.all_gather(projected, SEC)

    partial = gram(me, w_all)
    arrived = lax.all_to_all(partial.reshape(ndp, -1, R), DP, 0, 0, tiled=True)
    piece = jnp.sum(arrived.astype(F32), axis=0).astype(BF)
    line = lax.all_gather(piece, ("zh", "zl"), tiled=True)
    g = lax.all_gather(line, ("c", "y", "x"), tiled=True)

    coef = relay(axes, width, pxc, ss, g)
    mine = terms(me, ndp, inputs, cotangent, coef)
    arrived = lax.all_to_all(mine, DP, 0, 0, tiled=True)
    total = jnp.sum(arrived.astype(F32), axis=0)
    m_own = total[2 * slab :].astype(BF)
    m_all = lax.all_to_all(jnp.broadcast_to(m_own[None], (ndp,) + m_own.shape), DP, 0, 0, tiled=True)
    m_all = m_all.reshape(SECTIONS, 4 * R, R)
    diag_in, diag_out = finish(me, total[: 2 * slab], w_all, m_all)
    return diag_in[None], diag_out[None]


def solution(mesh, axes=(4, 2, 4, 4, 2)):
    fine = Mesh(mesh.devices.reshape(axes), SEC + DP)
    tokens, weights = P(DP, None), P(SEC, None, None)
    return jax.shard_map(
        functools.partial(on_device, axes),
        mesh=fine,
        in_specs=(tokens, tokens, weights, weights, weights, weights),
        out_specs=(P(SEC, DP, None), P(SEC, DP, None)),
        check_vma=False,
    )
```

```python
import functools

import jax
import jax.numpy as jnp
from jax import lax
from jax.experimental import pallas as pl
from jax.experimental.pallas import tpu as pltpu
from jax.sharding import Mesh, PartitionSpec as P

EPS = 1e-05
R = 128
SECTIONS = 8
BLOCKS = 16
SEC = ("zh", "c")
DP = ("y", "x", "zl")
BF = jnp.bfloat16
F32 = jnp.float32


def mm(left, right):
    return jnp.dot(left, right, preferred_element_type=F32)


def mm_nt(left, right):
    return lax.dot_general(left, right, (((1,), (1,)), ((), ())), preferred_element_type=F32)


def mm_tn(left, right):
    return lax.dot_general(left, right, (((0,), (0,)), ((), ())), preferred_element_type=F32)


def call(kernel, **kw):
    return pl.pallas_call(kernel, **kw)


def project_kernel(slab, pos_ref, x_ref, c_ref, a_ref, p_ref, b_ref, q_ref, *refs):
    out_ref, ss_ref, keep_x_ref, keep_c_ref, send_ref, acc, acc_ss = refs
    step = pl.program_id(0)

    @pl.when(step == 0)
    def _():
        acc[...] = jnp.zeros_like(acc)
        acc_ss[...] = jnp.zeros_like(acc_ss)

    x, c = x_ref[...], c_ref[...]
    rows, width = x.shape
    x32 = x.astype(F32)
    acc_ss[...] += jnp.sum(x32 * x32, axis=-1, keepdims=True)
    ap = jnp.concatenate([a_ref[0], p_ref[0]], axis=1)
    bq = jnp.concatenate([b_ref[0], q_ref[0]], axis=1)
    acc[:, : 2 * R] += mm(x, ap)
    both = mm(jnp.concatenate([x, c], axis=0), bq)
    acc[:, 2 * R : 4 * R] += both[:rows]
    acc[:, 4 * R :] += both[rows:]

    core, odd = pos_ref[1], pos_ref[4] == 1

    def split(value):
        pick = lambda n: jnp.concatenate(
            [value[:, k * slab : (k + 1) * slab] for k in range(n, width // slab, 2)], axis=1
        )
        first, second = pick(0), pick(1)
        return jnp.where(odd, second, first), jnp.where(odd, first, second)

    keep_x, send_x = split(x)
    keep_c, send_c = split(c)
    keep_x_ref[...] = keep_x
    keep_c_ref[...] = keep_c
    send_ref[...] = jnp.where(core == 0, send_x, send_c)

    @pl.when(step == pl.num_programs(0) - 1)
    def _():
        out_ref[...] = acc[...].astype(BF)
        ss_ref[...] = acc_ss[...]


def project(pos, slab, x, c, a, p, b, q):
    rows, width = x.shape
    steps = 4
    block = width // steps
    wide = pl.BlockSpec((rows, block), lambda k: (0, k))
    half = pl.BlockSpec((rows, block // 2), lambda k: (0, k))
    weight = pl.BlockSpec((1, block, R), lambda k: (0, k, 0))
    half_shape = jax.ShapeDtypeStruct((rows, width // 2), BF)
    return call(
        functools.partial(project_kernel, slab),
        grid=(steps,),
        in_specs=[pl.BlockSpec(memory_space=pltpu.SMEM)]
        + [wide, wide, weight, weight, weight, weight],
        out_specs=[
            pl.BlockSpec((rows, 6 * R), lambda k: (0, 0)),
            pl.BlockSpec((rows, R), lambda k: (0, 0)),
            half,
            half,
            half,
        ],
        out_shape=[
            jax.ShapeDtypeStruct((rows, 6 * R), BF),
            jax.ShapeDtypeStruct((rows, R), F32),
            half_shape,
            half_shape,
            half_shape,
        ],
        scratch_shapes=[pltpu.VMEM((rows, 6 * R), F32), pltpu.VMEM((rows, R), F32)],
        compiler_params=pltpu.CompilerParams(vmem_limit_bytes=60 * 1024 * 1024),
        cost_estimate=pl.CostEstimate(
            flops=2 * rows * width * 6 * R,
            bytes_accessed=4 * rows * width + 8 * width * R,
            transcendentals=0,
        ),
    )(pos, x, c, a, p, b, q)


def gram_kernel(pos_ref, own_ref, own_sib_ref, prev_ref, prev_sib_ref, next_ref, next_sib_ref, out_ref):
    chip, core = pos_ref[0], pos_ref[1]

    def cols(value, names):
        return jnp.concatenate([value[n] for n in names], axis=1)

    def four(low, high):
        from_b = mm_tn(low[2], cols(high, (0, 2, 1, 3)))
        from_q = mm_tn(low[3], cols(high, (0, 2)))
        mixed = from_b[:, 2 * R :] + from_q
        return [from_b[:, :R], from_b[:, R : 2 * R], mixed[:, :R], mixed[:, R:]]

    def put(at, block):
        out_ref[at * R : (at + 1) * R] = block.astype(BF)

    own, own_sib = own_ref[...], own_sib_ref[...]
    prev, prev_sib = prev_ref[...], prev_sib_ref[...]
    after, after_sib = next_ref[...], next_sib_ref[...]
    wrap = chip == 3
    for slot, other in enumerate((after, after_sib)):
        pair = four(jnp.where(wrap, other, own), jnp.where(wrap, own, other))
        for i in range(4):
            put(slot * 4 + i, pair[i])
    middle = (chip == 1) | (chip == 2)
    pair = four(jnp.where(middle, prev, after), jnp.where(middle, after, prev_sib))
    for i in range(4):
        put(8 + i, pair[i])
    first = core == 0
    pair = four(jnp.where(first, own, own_sib), jnp.where(first, own_sib, own))
    for i in range(2):
        put(12 + i, jnp.where(first, pair[i], pair[2 + i]))
    self_b = mm_tn(own[2], cols(own, (2, 3)))
    put(14, self_b[:, :R])
    put(15, self_b[:, R:] + mm_tn(own[3], own[2]))


def gram(pos, *slices):
    return call(
        gram_kernel,
        in_specs=[pl.BlockSpec(memory_space=pltpu.SMEM)]
        + [pl.BlockSpec(memory_space=pltpu.VMEM)] * 6,
        out_specs=pl.BlockSpec(memory_space=pltpu.VMEM),
        out_shape=jax.ShapeDtypeStruct((BLOCKS * R, R), BF),
        compiler_params=pltpu.CompilerParams(vmem_limit_bytes=60 * 1024 * 1024),
        cost_estimate=pl.CostEstimate(
            flops=2 * slices[0].shape[1] * BLOCKS * R * R,
            bytes_accessed=slices[0].size * 12,
            transcendentals=0,
        ),
    )(pos, *slices)


def place(low, high):
    gap = high // 2 - low // 2
    same = low % 2 == high % 2
    if gap == 0:
        return [(low, 12), (low, 13), (high, 12), (high, 13)]
    if gap == 2:
        chip = low // 2 + 1 if same else (low // 2 + 3) % 4
        return [(chip * 2 + low % 2, 8 + i) for i in range(4)]
    return [(low if gap == 1 else high, (0 if same else 4) + i) for i in range(4)]


def relay_kernel(axes, piece, width, pos_ref, ss_ref, *refs):
    nzh, nc, ny, nx, nzl = axes
    parts, (g_mine, g_sib, own_ref, m_ref, g, pxc, sem, sem_p, saved, coef) = refs[:8], refs[8:]
    chip, core = pos_ref[0], pos_ref[1]

    for n in range(8):
        section = lax.rem(chip + n // 2, nzh) * nc + (core if n % 2 == 0 else 1 - core)
        pltpu.make_async_copy(parts[n], pxc.at[section], sem_p).start()
    for source, c in ((g_mine, core), (g_sib, 1 - core)):

        def fetch(index, _):
            owner = lax.rem(index, nzh) * nc + c
            to = (owner * (ny * nx) + index // nzh) * piece
            pltpu.make_async_copy(
                source.at[pl.ds(pl.multiple_of(index * piece, 16), piece)],
                g.at[pl.ds(pl.multiple_of(to, 16), piece)],
                sem,
            ).start()
            return 0

        lax.fori_loop(0, nzh * ny * nx, fetch, 0)
    pltpu.make_async_copy(pxc, pxc, sem_p).wait()
    pltpu.make_async_copy(g, g, sem).wait()

    def block(at):
        start = (at[0] * BLOCKS + at[1]) * R
        return g[start : start + R]

    def pair(at):
        plain = jnp.concatenate([block(at[0]), block(at[1])], axis=1)
        return plain, jnp.concatenate([block(at[2]), block(at[3])], axis=1)

    rows = pxc.shape[1]
    ss = ss_ref[...][:, :1]
    st = jnp.zeros_like(ss)
    rsum = lambda v: jnp.sum(v, axis=-1, keepdims=True)
    hs, dhs, scales, mus = [], [], [], []
    for s in range(SECTIONS):
        base = pxc[s]
        xa, xd, xb, xs = [base[:, i * R : (i + 1) * R].astype(F32) for i in range(4)]
        for j in range(s):
            plain, mixed = pair(place(j, s))
            both = mm(jnp.concatenate([hs[j], dhs[j]], axis=0), plain)
            cross = mm(hs[j], mixed)
            xa = xa + both[:rows, :R]
            xb = xb + both[:rows, R:]
            xd = xd + (both[rows:, :R] + cross[:, :R])
            xs = xs + (both[rows:, R:] + cross[:, R:])
        r = lax.rsqrt(ss / width + EPS)
        mu = r * r * r * (st / width)
        pre = r * xa
        dpre = r * xd - mu * xa
        sig = 1.0 / (1.0 + jnp.exp(-pre))
        slope = sig * (1.0 + pre * (1.0 - sig))
        bend = sig * (1.0 - sig) * (2.0 + pre * (1.0 - 2.0 * sig))
        h = (pre * sig).astype(BF)
        dh = (slope * dpre).astype(BF)
        hs.append(h)
        dhs.append(dh)
        scales.append(r)
        mus.append(mu)
        same, cross = block((s, 14)), block((s, 15))
        both = mm(jnp.concatenate([h, dh], axis=0), same)
        turn = mm(h, cross)
        xb_new = xb + both[:rows]
        h32, dh32 = h.astype(F32), dh.astype(F32)
        ss = ss + rsum(h32 * (xb + xb_new))
        st = st + rsum(dh32 * xb_new + h32 * (xs + 0.5 * turn))
        xs_new = xs + turn + both[rows:]
        for i, value in enumerate((xa, xd, xb_new, xs_new, slope, bend * dpre)):
            saved[s, i] = value
        coef[s, 0] = h
        coef[s, 1] = dh

    total = jnp.zeros_like(ss)
    dtotal = jnp.zeros_like(ss)
    left, dleft = [None] * SECTIONS, [None] * SECTIONS
    for s in reversed(range(SECTIONS)):
        xa, xd, xb_new, xs_new, slope, curve = [saved[s, i] for i in range(6)]
        base = pxc[s]
        gh = base[:, 4 * R : 5 * R].astype(F32) - total * xb_new
        dgh = base[:, 5 * R :].astype(F32) - (dtotal * xb_new + total * xs_new)
        for i in range(s + 1, SECTIONS):
            plain, mixed = pair(place(s, i))
            both = mm_nt(jnp.concatenate([left[i], dleft[i]], axis=0), plain)
            gh = gh + both[:rows]
            dgh = dgh + (both[rows:] + mm_nt(left[i], mixed))
        ga = gh * slope
        dga = dgh * slope + gh * curve
        r, mu = scales[s], mus[s]
        u = (r * dga - mu * ga).astype(BF)
        v = (r * ga).astype(BF)
        h32, dh32 = hs[s].astype(F32), dhs[s].astype(F32)
        z = (-total * h32).astype(BF)
        y = (-(dtotal * h32 + total * dh32)).astype(BF)
        left[s] = jnp.concatenate([v, z], axis=1)
        dleft[s] = jnp.concatenate([u, y], axis=1)
        coef[s, 2] = u
        coef[s, 3] = v
        coef[s, 4] = z
        coef[s, 5] = y
        inner = rsum(ga * xa) / width
        dinner = rsum(dga * xa + ga * xd) / width
        total = total + r * r * r * inner
        dtotal = dtotal + r * r * r * dinner - 3.0 * r * r * mu * inner

    me = chip * nc + core
    h, dh, u, v, z, y = [coef[me, n] for n in range(6)]
    for n, value in enumerate((u, y, dh)):
        own_ref[n] = value

    ht, dht, ut, vt, zt, yt = [value.T for value in (h, dh, u, v, z, y)]

    def products(p0, p1, r0t, r1t):
        first = mm(jnp.concatenate([r0t, r1t], axis=1), jnp.concatenate([p0, p1], axis=0))
        return first, mm(r1t, p0)

    for i in range(SECTIONS):
        hi, dhi, ui, vi, zi, yi = [coef[i, n] for n in range(6)]
        below, upto = i < me, i <= me
        m0, m1 = products(
            jnp.where(below, hi, vi),
            jnp.where(below, dhi, ui),
            jnp.where(below, ut, dht),
            jnp.where(below, vt, ht),
        )
        m2, m3 = products(
            jnp.where(upto, hi, zi),
            jnp.where(upto, dhi, yi),
            jnp.where(upto, yt, dht),
            jnp.where(upto, zt, ht),
        )
        keep = i != me
        for n, m in enumerate((jnp.where(keep, m0, 0.0), jnp.where(keep, m1, 0.0), m2, m3)):
            m_ref[i * 4 + n] = m.astype(BF)


def relay(axes, width, pos, ss, parts, g_mine, g_sib):
    rows = ss.shape[0]
    total = 2 * g_mine.shape[0]
    piece = total // (axes[0] * axes[1] * axes[2] * axes[3])
    vm = pl.BlockSpec(memory_space=pltpu.VMEM)
    far = pl.BlockSpec(memory_space=pl.ANY)
    return call(
        functools.partial(relay_kernel, axes, piece, float(width)),
        in_specs=[pl.BlockSpec(memory_space=pltpu.SMEM), vm] + [far] * 10,
        out_specs=[vm, vm],
        out_shape=[
            jax.ShapeDtypeStruct((3, rows, R), BF),
            jax.ShapeDtypeStruct((4 * SECTIONS, R, R), BF),
        ],
        scratch_shapes=[
            pltpu.VMEM((total, R), BF),
            pltpu.VMEM((SECTIONS, rows, 6 * R), BF),
            pltpu.SemaphoreType.DMA,
            pltpu.SemaphoreType.DMA,
            pltpu.VMEM((SECTIONS, 6, rows, R), F32),
            pltpu.VMEM((SECTIONS, 6, rows, R), BF),
        ],
        compiler_params=pltpu.CompilerParams(vmem_limit_bytes=60 * 1024 * 1024),
        cost_estimate=pl.CostEstimate(
            flops=2 * 28 * 12 * rows * R * R, bytes_accessed=total * R * 2, transcendentals=0
        ),
    )(pos, ss, *parts, g_mine, g_sib)


def terms_kernel(pos_ref, x_ref, c_ref, recv_ref, sib_ref, own_ref, far_ref, out_ref):
    first = pos_ref[1] == 0
    part = out_ref.shape[0]
    slab = x_ref.shape[1] // part
    out_ref[:, 2 * slab :] = jnp.zeros_like(out_ref[:, 2 * slab :])
    recv, sib = recv_ref[...], sib_ref[...]
    x = jnp.concatenate([x_ref[...], jnp.where(first, recv, sib)], axis=0)
    c = jnp.concatenate([c_ref[...], jnp.where(first, sib, recv)], axis=0)
    u, y, dh = [jnp.concatenate([own_ref[n], far_ref[n]], axis=0) for n in range(3)]
    from_x = mm_tn(x, jnp.concatenate([u, y], axis=1))
    t_in = from_x[:, :R].astype(BF)
    t_out = (from_x[:, R:] + mm_tn(c, dh)).astype(BF)
    for n in range(part):
        out_ref[n, :slab] = t_in[n * slab : (n + 1) * slab]
        out_ref[n, slab : 2 * slab] = t_out[n * slab : (n + 1) * slab]


def terms(pos, slab, room, x, c, recv, recv_sib, own, far):
    rows, width = x.shape
    steps = 4
    block = width // steps
    wide = pl.BlockSpec((rows, block), lambda i: (0, i))
    small = pl.BlockSpec(own.shape, lambda i: (0, 0, 0))
    part = block // slab
    return call(
        terms_kernel,
        grid=(steps,),
        in_specs=[pl.BlockSpec(memory_space=pltpu.SMEM), wide, wide, wide, wide, small, small],
        out_specs=pl.BlockSpec((part, 2 * slab + room, R), lambda i: (i, 0, 0)),
        out_shape=jax.ShapeDtypeStruct((width // slab, 2 * slab + room, R), BF),
        compiler_params=pltpu.CompilerParams(vmem_limit_bytes=60 * 1024 * 1024),
        cost_estimate=pl.CostEstimate(
            flops=4 * rows * width * 3 * R, bytes_accessed=12 * rows * width, transcendentals=0
        ),
    )(pos, x, c, recv, recv_sib, own, far)


def finish_kernel(axes, pos_ref, all_ref, *refs):
    nzh, nc, ny, nx, nzl = axes
    slices, (in_ref, out_ref) = refs[:8], refs[8:]
    chip, core = pos_ref[0], pos_ref[1]
    me = nc * chip + core
    own = slices[0]
    slab = own.shape[1]
    each = 4 * SECTIONS // (ny * nx)
    t = all_ref[0, : 2 * slab].astype(F32)
    for n in range(1, ny * nx):
        t = t + all_ref[n, : 2 * slab].astype(F32)
    t_in, t_out = t[:slab], t[slab:]

    def m_block(at):
        row = 2 * slab + lax.rem(at, each) * R
        return all_ref[at // each, pl.ds(pl.multiple_of(row, 16), R)]

    for n in range(8):
        i = nc * lax.rem(chip + n // 2, nzh) + (core if n % 2 == 0 else 1 - core)
        below = i < me
        a, p, b, q = [slices[n][k] for k in range(4)]
        first = jnp.concatenate([jnp.where(below, b, a), jnp.where(below, q, p)], axis=1)
        ms = [m_block(i * 4 + k) for k in range(4)]
        product = mm_nt(first, jnp.concatenate(ms[:2], axis=1))
        t_in = t_in + jnp.where(below, product, 0.0)
        t_out = t_out + jnp.where(below, 0.0, product)
        t_out = t_out + mm_nt(jnp.concatenate([b, q], axis=1), jnp.concatenate(ms[2:], axis=1))
    in_ref[...] = own[1].astype(F32) * t_in
    out_ref[...] = own[3].astype(F32) * t_out


def finish(axes, pos, arrived, slices):
    vm = pl.BlockSpec(memory_space=pltpu.VMEM)
    shape = jax.ShapeDtypeStruct((slices[0].shape[1], R), F32)
    return call(
        functools.partial(finish_kernel, axes),
        in_specs=[pl.BlockSpec(memory_space=pltpu.SMEM)] + [vm] * 9,
        out_specs=[vm, vm],
        out_shape=[shape, shape],
        compiler_params=pltpu.CompilerParams(vmem_limit_bytes=60 * 1024 * 1024),
    )(pos, arrived, *slices)


def shifted(value, axis, steps):
    count = lax.axis_size(axis)
    return lax.ppermute(value, axis, [(i, (i + steps) % count) for i in range(count)])


def spread(value, axis):
    copies = jnp.broadcast_to(value[None], (lax.axis_size(axis),) + value.shape)
    return lax.all_to_all(copies, axis, 0, 0, tiled=True).reshape((-1,) + value.shape[1:])


def on_device(axes, inputs, cotangent, adapt_in, adapt_out, probe_in, probe_out):
    nzh, nc, ny, nx, nzl = axes
    ndp = ny * nx * nzl
    rows, width = inputs.shape
    slab = width // ndp
    pos = jnp.stack([lax.axis_index(n) for n in SEC + DP]).astype(jnp.int32)
    dp = lax.axis_index(DP)
    sib = lambda w: shifted(w, "c", 1)

    own = jnp.stack(
        [
            lax.dynamic_slice_in_dim(w[0], dp * slab, slab, 0)
            for w in (adapt_in, probe_in, adapt_out, probe_out)
        ]
    )
    prev, after = shifted(own, "zh", 1), shifted(own, "zh", -1)
    own_sib = sib(own)
    projected, ss, keep_x, keep_c, send = project(
        pos, slab, inputs, cotangent, adapt_in, probe_in, adapt_out, probe_out
    )
    prev, after, projected, send = lax.optimization_barrier((prev, after, projected, send))
    prev_sib, after_sib = sib(prev), sib(after)
    partial = gram(pos, own, own_sib, prev, prev_sib, after, after_sib)

    near = [projected] + [shifted(projected, "zh", -k) for k in (1, 2, 3)]
    recv = shifted(send, "zl", 1)
    opposite = shifted(own, "zh", 2)

    arrived = lax.all_to_all(partial.reshape(ny * nx, -1, R), ("y", "x"), 0, 0, tiled=True)
    arrived, near[1], near[3] = lax.optimization_barrier((arrived, near[1], near[3]))
    piece = jnp.sum(arrived.astype(F32), axis=0).astype(BF)
    line = spread(piece, ("zh", "zl")).reshape(nzh, nzl, -1, R)
    line = jnp.sum(line.astype(F32), axis=1).astype(BF).reshape(-1, R)
    g_mine = spread(line, ("y", "x"))
    g_mine, near = lax.optimization_barrier((g_mine, near))
    parts = [v for w in near for v in (w, sib(w))]
    g_sib = sib(g_mine)

    own3, m_part = relay(axes, width, pos, ss, parts, g_mine, g_sib)
    own3, recv = lax.optimization_barrier((own3, recv))
    far3 = shifted(own3, "zl", 1)
    m_arrived = lax.all_to_all(m_part.reshape(ny * nx, -1, R), ("y", "x"), 0, 0, tiled=True)
    m_own = jnp.sum(m_arrived.astype(F32), axis=0)
    room = m_own.shape[0]
    mine = terms(pos, slab, room, keep_x, keep_c, recv, sib(recv), own3, far3)
    m_own = (m_own + shifted(m_own, "zl", 1)).astype(BF)
    copies = jnp.broadcast_to(m_own[None], (ny * nx,) + m_own.shape)
    mine = lax.dynamic_update_slice(mine, copies, (0, 2 * slab, 0))
    arrived = lax.all_to_all(mine, ("y", "x"), 0, 0, tiled=True)
    arrived, opposite = lax.optimization_barrier((arrived, opposite))
    slices = [own, own_sib, after, after_sib, opposite, sib(opposite), prev, prev_sib]
    diag_in, diag_out = finish(axes, pos, arrived, slices)
    return diag_in[None], diag_out[None]


def solution(mesh, axes=(4, 2, 4, 4, 2)):
    fine = Mesh(mesh.devices.reshape(axes), SEC + DP)
    tokens, weights = P(DP, None), P(SEC, None, None)
    return jax.shard_map(
        functools.partial(on_device, axes),
        mesh=fine,
        in_specs=(tokens, tokens, weights, weights, weights, weights),
        out_specs=(P(SEC, DP, None), P(SEC, DP, None)),
        check_vma=False,
    )
```

```python
import functools

import jax
import jax.numpy as jnp
from jax import lax
from jax.experimental import pallas as pl
from jax.experimental.pallas import tpu as pltpu
from jax.sharding import Mesh, PartitionSpec as P

EPS = 1e-05
R = 128
SECTIONS = 8
BLOCKS = 16
SEC = ("zh", "c")
DP = ("y", "x", "zl")
BF = jnp.bfloat16
F32 = jnp.float32


def mm(left, right):
    return jnp.dot(left, right, preferred_element_type=F32)


def mm_nt(left, right):
    return lax.dot_general(left, right, (((1,), (1,)), ((), ())), preferred_element_type=F32)


def mm_tn(left, right):
    return lax.dot_general(left, right, (((0,), (0,)), ((), ())), preferred_element_type=F32)


def call(kernel, **kw):
    return pl.pallas_call(kernel, **kw)


def project_kernel(slab, pos_ref, x_ref, c_ref, a_ref, p_ref, b_ref, q_ref, *refs):
    out_ref, ss_ref, keep_x_ref, keep_c_ref, send_ref, acc, acc_ss = refs
    step = pl.program_id(0)

    @pl.when(step == 0)
    def _():
        acc[...] = jnp.zeros_like(acc)
        acc_ss[...] = jnp.zeros_like(acc_ss)

    x, c = x_ref[...], c_ref[...]
    rows, width = x.shape
    x32 = x.astype(F32)
    acc_ss[...] += jnp.sum(x32 * x32, axis=-1, keepdims=True)
    ap = jnp.concatenate([a_ref[0], p_ref[0]], axis=1)
    bq = jnp.concatenate([b_ref[0], q_ref[0]], axis=1)
    acc[:, : 2 * R] += mm(x, ap)
    both = mm(jnp.concatenate([x, c], axis=0), bq)
    acc[:, 2 * R : 4 * R] += both[:rows]
    acc[:, 4 * R :] += both[rows:]

    core, odd = pos_ref[1], pos_ref[4] == 1

    def split(value):
        pick = lambda n: jnp.concatenate(
            [value[:, k * slab : (k + 1) * slab] for k in range(n, width // slab, 2)], axis=1
        )
        first, second = pick(0), pick(1)
        return jnp.where(odd, second, first), jnp.where(odd, first, second)

    keep_x, send_x = split(x)
    keep_c, send_c = split(c)
    keep_x_ref[...] = keep_x
    keep_c_ref[...] = keep_c
    send_ref[...] = jnp.where(core == 0, send_x, send_c)

    @pl.when(step == pl.num_programs(0) - 1)
    def _():
        out_ref[...] = acc[...].astype(BF)
        ss_ref[...] = acc_ss[...]


def project(pos, slab, x, c, a, p, b, q):
    rows, width = x.shape
    steps = 4
    block = width // steps
    wide = pl.BlockSpec((rows, block), lambda k: (0, k))
    half = pl.BlockSpec((rows, block // 2), lambda k: (0, k))
    weight = pl.BlockSpec((1, block, R), lambda k: (0, k, 0))
    half_shape = jax.ShapeDtypeStruct((rows, width // 2), BF)
    return call(
        functools.partial(project_kernel, slab),
        grid=(steps,),
        in_specs=[pl.BlockSpec(memory_space=pltpu.SMEM)]
        + [wide, wide, weight, weight, weight, weight],
        out_specs=[
            pl.BlockSpec((rows, 6 * R), lambda k: (0, 0)),
            pl.BlockSpec((rows, R), lambda k: (0, 0)),
            half,
            half,
            half,
        ],
        out_shape=[
            jax.ShapeDtypeStruct((rows, 6 * R), BF),
            jax.ShapeDtypeStruct((rows, R), F32),
            half_shape,
            half_shape,
            half_shape,
        ],
        scratch_shapes=[pltpu.VMEM((rows, 6 * R), F32), pltpu.VMEM((rows, R), F32)],
        compiler_params=pltpu.CompilerParams(vmem_limit_bytes=60 * 1024 * 1024),
        cost_estimate=pl.CostEstimate(
            flops=2 * rows * width * 6 * R,
            bytes_accessed=4 * rows * width + 8 * width * R,
            transcendentals=0,
        ),
    )(pos, x, c, a, p, b, q)


def gram_kernel(pos_ref, own_ref, own_sib_ref, prev_ref, prev_sib_ref, next_ref, next_sib_ref, out_ref):
    chip, core = pos_ref[0], pos_ref[1]

    def cols(value, names):
        return jnp.concatenate([value[n] for n in names], axis=1)

    def four(low, high):
        from_b = mm_tn(low[2], cols(high, (0, 2, 1, 3)))
        from_q = mm_tn(low[3], cols(high, (0, 2)))
        mixed = from_b[:, 2 * R :] + from_q
        return [from_b[:, :R], from_b[:, R : 2 * R], mixed[:, :R], mixed[:, R:]]

    def put(at, block):
        out_ref[at * R : (at + 1) * R] = block.astype(BF)

    own, own_sib = own_ref[...], own_sib_ref[...]
    prev, prev_sib = prev_ref[...], prev_sib_ref[...]
    after, after_sib = next_ref[...], next_sib_ref[...]
    wrap = chip == 3
    for slot, other in enumerate((after, after_sib)):
        pair = four(jnp.where(wrap, other, own), jnp.where(wrap, own, other))
        for i in range(4):
            put(slot * 4 + i, pair[i])
    middle = (chip == 1) | (chip == 2)
    pair = four(jnp.where(middle, prev, after), jnp.where(middle, after, prev_sib))
    for i in range(4):
        put(8 + i, pair[i])
    first = core == 0
    pair = four(jnp.where(first, own, own_sib), jnp.where(first, own_sib, own))
    for i in range(2):
        put(12 + i, jnp.where(first, pair[i], pair[2 + i]))
    self_b = mm_tn(own[2], cols(own, (2, 3)))
    put(14, self_b[:, :R])
    put(15, self_b[:, R:] + mm_tn(own[3], own[2]))


def gram(pos, *slices):
    return call(
        gram_kernel,
        in_specs=[pl.BlockSpec(memory_space=pltpu.SMEM)]
        + [pl.BlockSpec(memory_space=pltpu.VMEM)] * 6,
        out_specs=pl.BlockSpec(memory_space=pltpu.VMEM),
        out_shape=jax.ShapeDtypeStruct((BLOCKS * R, R), BF),
        compiler_params=pltpu.CompilerParams(vmem_limit_bytes=60 * 1024 * 1024),
        cost_estimate=pl.CostEstimate(
            flops=2 * slices[0].shape[1] * BLOCKS * R * R,
            bytes_accessed=slices[0].size * 12,
            transcendentals=0,
        ),
    )(pos, *slices)


def place(low, high):
    gap = high // 2 - low // 2
    same = low % 2 == high % 2
    if gap == 0:
        return [(low, 12), (low, 13), (high, 12), (high, 13)]
    if gap == 2:
        chip = low // 2 + 1 if same else (low // 2 + 3) % 4
        return [(chip * 2 + low % 2, 8 + i) for i in range(4)]
    return [(low if gap == 1 else high, (0 if same else 4) + i) for i in range(4)]


def relay_kernel(axes, piece, width, pos_ref, ss_ref, *refs):
    nzh, nc, ny, nx, nzl = axes
    parts, (g_mine, g_sib, own_ref, m_ref, g, pxc, sem, sem_p, saved, coef) = refs[:8], refs[8:]
    chip, core = pos_ref[0], pos_ref[1]

    for n in range(8):
        section = lax.rem(chip + n // 2, nzh) * nc + (core if n % 2 == 0 else 1 - core)
        pltpu.make_async_copy(parts[n], pxc.at[section], sem_p).start()
    for source, c in ((g_mine, core), (g_sib, 1 - core)):

        def fetch(index, _):
            owner = lax.rem(chip + index, nzh) * nc + c
            to = (owner * (ny * nx) + index // nzh) * piece
            pltpu.make_async_copy(
                source.at[pl.ds(pl.multiple_of(index * piece, 16), piece)],
                g.at[pl.ds(pl.multiple_of(to, 16), piece)],
                sem,
            ).start()
            return 0

        lax.fori_loop(0, nzh * ny * nx, fetch, 0)
    pltpu.make_async_copy(pxc, pxc, sem_p).wait()
    pltpu.make_async_copy(g, g, sem).wait()

    def block(at):
        start = (at[0] * BLOCKS + at[1]) * R
        return g[start : start + R]

    def pair(at):
        plain = jnp.concatenate([block(at[0]), block(at[1])], axis=1)
        return plain, jnp.concatenate([block(at[2]), block(at[3])], axis=1)

    rows = pxc.shape[1]
    ss = ss_ref[...][:, :1]
    st = jnp.zeros_like(ss)
    rsum = lambda v: jnp.sum(v, axis=-1, keepdims=True)
    hs, dhs, scales, mus = [], [], [], []
    sums = [[pxc[s, :, i * R : (i + 1) * R].astype(F32) for i in range(4)] for s in range(SECTIONS)]
    for s in range(SECTIONS):
        xa, xd, xb, xs = sums[s]
        r = lax.rsqrt(ss / width + EPS)
        mu = r * r * r * (st / width)
        pre = r * xa
        dpre = r * xd - mu * xa
        sig = 1.0 / (1.0 + jnp.exp(-pre))
        slope = sig * (1.0 + pre * (1.0 - sig))
        h = (pre * sig).astype(BF)
        dh = (slope * dpre).astype(BF)
        hs.append(h)
        dhs.append(dh)
        scales.append(r)
        mus.append(mu)
        coef[s, 0] = h
        coef[s, 1] = dh
        stacked = jnp.concatenate([h, dh], axis=0)
        both = mm(stacked, block((s, 14)))
        turn = mm(h, block((s, 15)))
        xb_new = xb + both[:rows]
        xs_new = xs + turn + both[rows:]
        h32, dh32 = h.astype(F32), dh.astype(F32)
        ss = ss + rsum(h32 * (xb + xb_new))
        st = st + rsum(dh32 * xb_new + h32 * (xs + 0.5 * turn))
        for later in range(s + 1, SECTIONS):
            plain, mixed = pair(place(s, later))
            both = mm(stacked, plain)
            cross = mm(h, mixed)
            la, ld, lb, ls = sums[later]
            sums[later] = [
                la + both[:rows, :R],
                ld + (both[rows:, :R] + cross[:, :R]),
                lb + both[:rows, R:],
                ls + (both[rows:, R:] + cross[:, R:]),
            ]
        bend = sig * (1.0 - sig) * (2.0 + pre * (1.0 - 2.0 * sig))
        for i, value in enumerate((xa, xd, xb_new, xs_new, slope, bend * dpre)):
            saved[s, i] = value

    total = jnp.zeros_like(ss)
    dtotal = jnp.zeros_like(ss)
    back = [[pxc[s, :, i * R : (i + 1) * R].astype(F32) for i in (4, 5)] for s in range(SECTIONS)]
    for s in reversed(range(SECTIONS)):
        xa, xd, xb_new, xs_new, slope, curve = [saved[s, i] for i in range(6)]
        gh = back[s][0] - total * xb_new
        dgh = back[s][1] - (dtotal * xb_new + total * xs_new)
        ga = gh * slope
        dga = dgh * slope + gh * curve
        r, mu = scales[s], mus[s]
        u = (r * dga - mu * ga).astype(BF)
        v = (r * ga).astype(BF)
        h32, dh32 = hs[s].astype(F32), dhs[s].astype(F32)
        z = (-total * h32).astype(BF)
        y = (-(dtotal * h32 + total * dh32)).astype(BF)
        left = jnp.concatenate([v, z], axis=1)
        stacked = jnp.concatenate([left, jnp.concatenate([u, y], axis=1)], axis=0)
        for early in reversed(range(s)):
            plain, mixed = pair(place(early, s))
            both = mm_nt(stacked, plain)
            gh, dgh = back[early]
            back[early] = [gh + both[:rows], dgh + (both[rows:] + mm_nt(left, mixed))]
        for n, value in enumerate((u, v, z, y)):
            coef[s, 2 + n] = value
        inner = rsum(ga * xa) / width
        dinner = rsum(dga * xa + ga * xd) / width
        total = total + r * r * r * inner
        dtotal = dtotal + r * r * r * dinner - 3.0 * r * r * mu * inner

    me = chip * nc + core
    h, dh, u, v, z, y = [coef[me, n] for n in range(6)]
    for n, value in enumerate((u, y, dh)):
        own_ref[n] = value

    ht, dht, ut, vt, zt, yt = [value.T for value in (h, dh, u, v, z, y)]

    def products(p0, p1, r0t, r1t):
        first = mm(jnp.concatenate([r0t, r1t], axis=1), jnp.concatenate([p0, p1], axis=0))
        return first, mm(r1t, p0)

    for i in range(SECTIONS):
        hi, dhi, ui, vi, zi, yi = [coef[i, n] for n in range(6)]
        below, upto = i < me, i <= me
        m0, m1 = products(
            jnp.where(below, hi, vi),
            jnp.where(below, dhi, ui),
            jnp.where(below, ut, dht),
            jnp.where(below, vt, ht),
        )
        m2, m3 = products(
            jnp.where(upto, hi, zi),
            jnp.where(upto, dhi, yi),
            jnp.where(upto, yt, dht),
            jnp.where(upto, zt, ht),
        )
        keep = i != me
        for n, m in enumerate((jnp.where(keep, m0, 0.0), jnp.where(keep, m1, 0.0), m2, m3)):
            m_ref[i * 4 + n] = m.astype(BF)


def relay(axes, width, pos, ss, parts, g_mine, g_sib):
    rows = ss.shape[0]
    total = 2 * g_mine.shape[0]
    piece = total // (axes[0] * axes[1] * axes[2] * axes[3])
    vm = pl.BlockSpec(memory_space=pltpu.VMEM)
    far = pl.BlockSpec(memory_space=pl.ANY)
    return call(
        functools.partial(relay_kernel, axes, piece, float(width)),
        in_specs=[pl.BlockSpec(memory_space=pltpu.SMEM), vm] + [far] * 10,
        out_specs=[vm, vm],
        out_shape=[
            jax.ShapeDtypeStruct((3, rows, R), BF),
            jax.ShapeDtypeStruct((4 * SECTIONS, R, R), BF),
        ],
        scratch_shapes=[
            pltpu.VMEM((total, R), BF),
            pltpu.VMEM((SECTIONS, rows, 6 * R), BF),
            pltpu.SemaphoreType.DMA,
            pltpu.SemaphoreType.DMA,
            pltpu.VMEM((SECTIONS, 6, rows, R), F32),
            pltpu.VMEM((SECTIONS, 6, rows, R), BF),
        ],
        compiler_params=pltpu.CompilerParams(vmem_limit_bytes=60 * 1024 * 1024),
        cost_estimate=pl.CostEstimate(
            flops=2 * 28 * 12 * rows * R * R, bytes_accessed=total * R * 2, transcendentals=0
        ),
    )(pos, ss, *parts, g_mine, g_sib)


def terms_kernel(pos_ref, x_ref, c_ref, recv_ref, sib_ref, own_ref, far_ref, out_ref):
    first = pos_ref[1] == 0
    part = out_ref.shape[0]
    slab = x_ref.shape[1] // part
    recv, sib = recv_ref[...], sib_ref[...]
    x = jnp.concatenate([x_ref[...], jnp.where(first, recv, sib)], axis=0)
    c = jnp.concatenate([c_ref[...], jnp.where(first, sib, recv)], axis=0)
    u, y, dh = [jnp.concatenate([own_ref[n], far_ref[n]], axis=0) for n in range(3)]
    from_x = mm_tn(x, jnp.concatenate([u, y], axis=1))
    t_in = from_x[:, :R].astype(BF)
    t_out = (from_x[:, R:] + mm_tn(c, dh)).astype(BF)
    for n in range(part):
        out_ref[n, :slab] = t_in[n * slab : (n + 1) * slab]
        out_ref[n, slab : 2 * slab] = t_out[n * slab : (n + 1) * slab]


def terms(pos, slab, room, x, c, recv, recv_sib, own, far):
    rows, width = x.shape
    steps = 4
    block = width // steps
    wide = pl.BlockSpec((rows, block), lambda i: (0, i))
    small = pl.BlockSpec(own.shape, lambda i: (0, 0, 0))
    part = block // slab
    return call(
        terms_kernel,
        grid=(steps,),
        in_specs=[pl.BlockSpec(memory_space=pltpu.SMEM), wide, wide, wide, wide, small, small],
        out_specs=pl.BlockSpec((part, 2 * slab + room, R), lambda i: (i, 0, 0)),
        out_shape=jax.ShapeDtypeStruct((width // slab, 2 * slab + room, R), BF),
        compiler_params=pltpu.CompilerParams(vmem_limit_bytes=60 * 1024 * 1024),
        cost_estimate=pl.CostEstimate(
            flops=4 * rows * width * 3 * R, bytes_accessed=12 * rows * width, transcendentals=0
        ),
    )(pos, x, c, recv, recv_sib, own, far)


def finish_kernel(axes, pos_ref, all_ref, *refs):
    nzh, nc, ny, nx, nzl = axes
    slices, (in_ref, out_ref) = refs[:8], refs[8:]
    chip, core = pos_ref[0], pos_ref[1]
    me = nc * chip + core
    own = slices[0]
    slab = own.shape[1]
    each = 4 * SECTIONS // (ny * nx)
    t = all_ref[0, : 2 * slab].astype(F32)
    for n in range(1, ny * nx):
        t = t + all_ref[n, : 2 * slab].astype(F32)
    t_in, t_out = t[:slab], t[slab:]

    def m_block(at):
        row = 2 * slab + lax.rem(at, each) * R
        return all_ref[at // each, pl.ds(pl.multiple_of(row, 16), R)]

    for n in range(8):
        i = nc * lax.rem(chip + n // 2, nzh) + (core if n % 2 == 0 else 1 - core)
        below = i < me
        a, p, b, q = [slices[n][k] for k in range(4)]
        first = jnp.concatenate([jnp.where(below, b, a), jnp.where(below, q, p)], axis=1)
        ms = [m_block(i * 4 + k) for k in range(4)]
        product = mm_nt(first, jnp.concatenate(ms[:2], axis=1))
        t_in = t_in + jnp.where(below, product, 0.0)
        t_out = t_out + jnp.where(below, 0.0, product)
        t_out = t_out + mm_nt(jnp.concatenate([b, q], axis=1), jnp.concatenate(ms[2:], axis=1))
    in_ref[...] = own[1].astype(F32) * t_in
    out_ref[...] = own[3].astype(F32) * t_out


def finish(axes, pos, arrived, slices):
    vm = pl.BlockSpec(memory_space=pltpu.VMEM)
    shape = jax.ShapeDtypeStruct((slices[0].shape[1], R), F32)
    return call(
        functools.partial(finish_kernel, axes),
        in_specs=[pl.BlockSpec(memory_space=pltpu.SMEM)] + [vm] * 9,
        out_specs=[vm, vm],
        out_shape=[shape, shape],
        compiler_params=pltpu.CompilerParams(vmem_limit_bytes=60 * 1024 * 1024),
    )(pos, arrived, *slices)


def shifted(value, axis, steps):
    count = lax.axis_size(axis)
    return lax.ppermute(value, axis, [(i, (i + steps) % count) for i in range(count)])


def spread(value, axis):
    copies = jnp.broadcast_to(value[None], (lax.axis_size(axis),) + value.shape)
    return lax.all_to_all(copies, axis, 0, 0, tiled=True).reshape((-1,) + value.shape[1:])


def on_device(axes, inputs, cotangent, adapt_in, adapt_out, probe_in, probe_out):
    nzh, nc, ny, nx, nzl = axes
    ndp = ny * nx * nzl
    rows, width = inputs.shape
    slab = width // ndp
    pos = jnp.stack([lax.axis_index(n) for n in SEC + DP]).astype(jnp.int32)
    dp = lax.axis_index(DP)
    sib = lambda w: shifted(w, "c", 1)

    own = jnp.stack(
        [
            lax.dynamic_slice_in_dim(w[0], dp * slab, slab, 0)
            for w in (adapt_in, probe_in, adapt_out, probe_out)
        ]
    )
    prev, after = shifted(own, "zh", 1), shifted(own, "zh", -1)
    own_sib = sib(own)
    projected, ss, keep_x, keep_c, send = project(
        pos, slab, inputs, cotangent, adapt_in, probe_in, adapt_out, probe_out
    )
    prev, after, projected, send = lax.optimization_barrier((prev, after, projected, send))
    prev_sib, after_sib = sib(prev), sib(after)
    partial = gram(pos, own, own_sib, prev, prev_sib, after, after_sib)

    recv = shifted(send, "zl", 1)

    arrived = lax.all_to_all(partial.reshape(ny * nx, -1, R), ("y", "x"), 0, 0, tiled=True)
    arrived, projected = lax.optimization_barrier((arrived, projected))
    near = [projected] + [shifted(projected, "zh", -k) for k in (1, 2, 3)]
    piece = jnp.sum(arrived.astype(F32), axis=0).astype(BF)
    piece = (piece.astype(F32) + shifted(piece, "zl", 1).astype(F32)).astype(BF)
    line = jnp.concatenate([piece] + [shifted(piece, "zh", -k) for k in (1, 2, 3)], axis=0)
    line, recv = lax.optimization_barrier((line, recv))
    g_mine = spread(line, ("y", "x"))
    projected_sib = sib(projected)
    g_mine, near[1:], projected_sib, prev = lax.optimization_barrier(
        (g_mine, near[1:], projected_sib, prev)
    )
    opposite = shifted(prev, "zh", 1)
    parts = [projected, projected_sib] + [v for w in near[1:] for v in (w, sib(w))]
    g_sib = sib(g_mine)

    own3, m_part = relay(axes, width, pos, ss, parts, g_mine, g_sib)
    own3, m_part, opposite = lax.optimization_barrier((own3, m_part, opposite))
    far3 = shifted(own3, "zl", 1)
    m_arrived = lax.all_to_all(m_part.reshape(ny * nx, -1, R), ("y", "x"), 0, 0, tiled=True)
    room = m_arrived.shape[1]
    mine = terms(pos, slab, room, keep_x, keep_c, recv, sib(recv), own3, far3)
    m_arrived, mine = lax.optimization_barrier((m_arrived, mine))
    opposite_sib = sib(opposite)
    m_own = jnp.sum(m_arrived.astype(F32), axis=0)
    m_own = (m_own + shifted(m_own, "zl", 1)).astype(BF)
    copies = jnp.broadcast_to(m_own[None], (ny * nx,) + m_own.shape)
    mine = lax.dynamic_update_slice(mine, copies, (0, 2 * slab, 0))
    mine, opposite_sib = lax.optimization_barrier((mine, opposite_sib))
    arrived = lax.all_to_all(mine, ("y", "x"), 0, 0, tiled=True)
    slices = [own, own_sib, after, after_sib, opposite, opposite_sib, prev, prev_sib]
    diag_in, diag_out = finish(axes, pos, arrived, slices)
    return diag_in[None], diag_out[None]


def solution(mesh, axes=(4, 2, 4, 4, 2)):
    fine = Mesh(mesh.devices.reshape(axes), SEC + DP)
    tokens, weights = P(DP, None), P(SEC, None, None)
    return jax.shard_map(
        functools.partial(on_device, axes),
        mesh=fine,
        in_specs=(tokens, tokens, weights, weights, weights, weights),
        out_specs=(P(SEC, DP, None), P(SEC, DP, None)),
        check_vma=False,
    )
```

```python
import functools

import jax
import jax.numpy as jnp
from jax import lax
from jax.experimental import pallas as pl
from jax.experimental.pallas import tpu as pltpu
from jax.sharding import Mesh, PartitionSpec as P

EPS = 1e-05
R = 128
SECTIONS = 8
BLOCKS = 16
SEC = ("zh", "c")
DP = ("y", "x", "zl")
BF = jnp.bfloat16
F32 = jnp.float32


def mm(left, right):
    return jnp.dot(left, right, preferred_element_type=F32)


def mm_nt(left, right):
    return lax.dot_general(left, right, (((1,), (1,)), ((), ())), preferred_element_type=F32)


def mm_tn(left, right):
    return lax.dot_general(left, right, (((0,), (0,)), ((), ())), preferred_element_type=F32)


def call(kernel, **kw):
    return pl.pallas_call(kernel, **kw)


def project_kernel(slab, pos_ref, x_ref, c_ref, a_ref, p_ref, b_ref, q_ref, *refs):
    out_ref, ss_ref, keep_x_ref, keep_c_ref, send_ref, acc, acc_ss = refs
    step = pl.program_id(0)

    @pl.when(step == 0)
    def _():
        acc[...] = jnp.zeros_like(acc)
        acc_ss[...] = jnp.zeros_like(acc_ss)

    x, c = x_ref[...], c_ref[...]
    rows, width = x.shape
    x32 = x.astype(F32)
    acc_ss[...] += jnp.sum(x32 * x32, axis=-1, keepdims=True)
    ap = jnp.concatenate([a_ref[0], p_ref[0]], axis=1)
    bq = jnp.concatenate([b_ref[0], q_ref[0]], axis=1)
    acc[:, : 2 * R] += mm(x, ap)
    both = mm(jnp.concatenate([x, c], axis=0), bq)
    acc[:, 2 * R : 4 * R] += both[:rows]
    acc[:, 4 * R :] += both[rows:]

    core, odd = pos_ref[1], pos_ref[4] == 1

    def split(value):
        pick = lambda n: jnp.concatenate(
            [value[:, k * slab : (k + 1) * slab] for k in range(n, width // slab, 2)], axis=1
        )
        first, second = pick(0), pick(1)
        return jnp.where(odd, second, first), jnp.where(odd, first, second)

    keep_x, send_x = split(x)
    keep_c, send_c = split(c)
    keep_x_ref[...] = keep_x
    keep_c_ref[...] = keep_c
    send_ref[...] = jnp.where(core == 0, send_x, send_c)

    @pl.when(step == pl.num_programs(0) - 1)
    def _():
        out_ref[...] = acc[...].astype(BF)
        ss_ref[...] = acc_ss[...]


def project(pos, slab, x, c, a, p, b, q):
    rows, width = x.shape
    steps = 4
    block = width // steps
    wide = pl.BlockSpec((rows, block), lambda k: (0, k))
    half = pl.BlockSpec((rows, block // 2), lambda k: (0, k))
    weight = pl.BlockSpec((1, block, R), lambda k: (0, k, 0))
    half_shape = jax.ShapeDtypeStruct((rows, width // 2), BF)
    return call(
        functools.partial(project_kernel, slab),
        grid=(steps,),
        in_specs=[pl.BlockSpec(memory_space=pltpu.SMEM)]
        + [wide, wide, weight, weight, weight, weight],
        out_specs=[
            pl.BlockSpec((rows, 6 * R), lambda k: (0, 0)),
            pl.BlockSpec((rows, R), lambda k: (0, 0)),
            half,
            half,
            half,
        ],
        out_shape=[
            jax.ShapeDtypeStruct((rows, 6 * R), BF),
            jax.ShapeDtypeStruct((rows, R), F32),
            half_shape,
            half_shape,
            half_shape,
        ],
        scratch_shapes=[pltpu.VMEM((rows, 6 * R), F32), pltpu.VMEM((rows, R), F32)],
        compiler_params=pltpu.CompilerParams(vmem_limit_bytes=60 * 1024 * 1024),
        cost_estimate=pl.CostEstimate(
            flops=2 * rows * width * 6 * R,
            bytes_accessed=4 * rows * width + 8 * width * R,
            transcendentals=0,
        ),
    )(pos, x, c, a, p, b, q)


def gram_kernel(pos_ref, own_ref, own_sib_ref, prev_ref, prev_sib_ref, next_ref, next_sib_ref, out_ref):
    chip, core = pos_ref[0], pos_ref[1]

    def cols(value, names):
        return jnp.concatenate([value[n] for n in names], axis=1)

    def four(low, high):
        from_b = mm_tn(low[2], cols(high, (0, 2, 1, 3)))
        from_q = mm_tn(low[3], cols(high, (0, 2)))
        mixed = from_b[:, 2 * R :] + from_q
        return [from_b[:, :R], from_b[:, R : 2 * R], mixed[:, :R], mixed[:, R:]]

    def put(at, block):
        out_ref[at * R : (at + 1) * R] = block.astype(BF)

    own, own_sib = own_ref[...], own_sib_ref[...]
    prev, prev_sib = prev_ref[...], prev_sib_ref[...]
    after, after_sib = next_ref[...], next_sib_ref[...]
    wrap = chip == 3
    for slot, other in enumerate((after, after_sib)):
        pair = four(jnp.where(wrap, other, own), jnp.where(wrap, own, other))
        for i in range(4):
            put(slot * 4 + i, pair[i])
    middle = (chip == 1) | (chip == 2)
    pair = four(jnp.where(middle, prev, after), jnp.where(middle, after, prev_sib))
    for i in range(4):
        put(8 + i, pair[i])
    first = core == 0
    pair = four(jnp.where(first, own, own_sib), jnp.where(first, own_sib, own))
    for i in range(2):
        put(12 + i, jnp.where(first, pair[i], pair[2 + i]))
    self_b = mm_tn(own[2], cols(own, (2, 3)))
    put(14, self_b[:, :R])
    put(15, self_b[:, R:] + mm_tn(own[3], own[2]))


def gram(pos, *slices):
    return call(
        gram_kernel,
        in_specs=[pl.BlockSpec(memory_space=pltpu.SMEM)]
        + [pl.BlockSpec(memory_space=pltpu.VMEM)] * 6,
        out_specs=pl.BlockSpec(memory_space=pltpu.VMEM),
        out_shape=jax.ShapeDtypeStruct((BLOCKS * R, R), BF),
        compiler_params=pltpu.CompilerParams(vmem_limit_bytes=60 * 1024 * 1024),
        cost_estimate=pl.CostEstimate(
            flops=2 * slices[0].shape[1] * BLOCKS * R * R,
            bytes_accessed=slices[0].size * 12,
            transcendentals=0,
        ),
    )(pos, *slices)


def place(low, high):
    gap = high // 2 - low // 2
    same = low % 2 == high % 2
    if gap == 0:
        return [(low, 12), (low, 13), (high, 12), (high, 13)]
    if gap == 2:
        chip = low // 2 + 1 if same else (low // 2 + 3) % 4
        return [(chip * 2 + low % 2, 8 + i) for i in range(4)]
    return [(low if gap == 1 else high, (0 if same else 4) + i) for i in range(4)]


def relay_kernel(axes, piece, width, pos_ref, ss_ref, *refs):
    nzh, nc, ny, nx, nzl = axes
    parts, (g_mine, g_sib, own_ref, m_ref, g, pxc, sem, sem_p, saved, coef) = refs[:8], refs[8:]
    chip, core = pos_ref[0], pos_ref[1]

    for n in range(8):
        section = lax.rem(chip + n // 2, nzh) * nc + (core if n % 2 == 0 else 1 - core)
        pltpu.make_async_copy(parts[n], pxc.at[section], sem_p).start()
    for source, c in ((g_mine, core), (g_sib, 1 - core)):

        def fetch(index, _):
            owner = lax.rem(chip + index, nzh) * nc + c
            to = (owner * (ny * nx) + index // nzh) * piece
            pltpu.make_async_copy(
                source.at[pl.ds(pl.multiple_of(index * piece, 16), piece)],
                g.at[pl.ds(pl.multiple_of(to, 16), piece)],
                sem,
            ).start()
            return 0

        lax.fori_loop(0, nzh * ny * nx, fetch, 0)
    pltpu.make_async_copy(pxc, pxc, sem_p).wait()
    pltpu.make_async_copy(g, g, sem).wait()

    def block(at):
        start = (at[0] * BLOCKS + at[1]) * R
        return g[start : start + R]

    def pair(at):
        plain = jnp.concatenate([block(at[0]), block(at[1])], axis=1)
        return plain, jnp.concatenate([block(at[2]), block(at[3])], axis=1)

    rows = pxc.shape[1]
    ss = ss_ref[...][:, :1]
    st = jnp.zeros_like(ss)
    rsum = lambda v: jnp.sum(v, axis=-1, keepdims=True)
    hs, dhs, scales, mus = [], [], [], []
    sums = [[pxc[s, :, i * R : (i + 1) * R].astype(F32) for i in range(4)] for s in range(SECTIONS)]
    for s in range(SECTIONS):
        xa, xd, xb, xs = sums[s]
        r = lax.rsqrt(ss / width + EPS)
        mu = r * r * r * (st / width)
        pre = r * xa
        dpre = r * xd - mu * xa
        sig = 1.0 / (1.0 + jnp.exp(-pre))
        slope = sig * (1.0 + pre * (1.0 - sig))
        h = (pre * sig).astype(BF)
        dh = (slope * dpre).astype(BF)
        hs.append(h)
        dhs.append(dh)
        scales.append(r)
        mus.append(mu)
        coef[s, 0] = h
        coef[s, 1] = dh
        stacked = jnp.concatenate([h, dh], axis=0)
        both = mm(stacked, block((s, 14)))
        turn = mm(h, block((s, 15)))
        xb_new = xb + both[:rows]
        xs_new = xs + turn + both[rows:]
        h32, dh32 = h.astype(F32), dh.astype(F32)
        ss = ss + rsum(h32 * (xb + xb_new))
        st = st + rsum(dh32 * xb_new + h32 * (xs + 0.5 * turn))
        for later in range(s + 1, SECTIONS):
            plain, mixed = pair(place(s, later))
            both = mm(stacked, plain)
            cross = mm(h, mixed)
            la, ld, lb, ls = sums[later]
            sums[later] = [
                la + both[:rows, :R],
                ld + (both[rows:, :R] + cross[:, :R]),
                lb + both[:rows, R:],
                ls + (both[rows:, R:] + cross[:, R:]),
            ]
        bend = sig * (1.0 - sig) * (2.0 + pre * (1.0 - 2.0 * sig))
        for i, value in enumerate((xa, xd, xb_new, xs_new, slope, bend * dpre)):
            saved[s, i] = value

    total = jnp.zeros_like(ss)
    dtotal = jnp.zeros_like(ss)
    back = [[pxc[s, :, i * R : (i + 1) * R].astype(F32) for i in (4, 5)] for s in range(SECTIONS)]
    for s in reversed(range(SECTIONS)):
        xa, xd, xb_new, xs_new, slope, curve = [saved[s, i] for i in range(6)]
        gh = back[s][0] - total * xb_new
        dgh = back[s][1] - (dtotal * xb_new + total * xs_new)
        ga = gh * slope
        dga = dgh * slope + gh * curve
        r, mu = scales[s], mus[s]
        u = (r * dga - mu * ga).astype(BF)
        v = (r * ga).astype(BF)
        h32, dh32 = hs[s].astype(F32), dhs[s].astype(F32)
        z = (-total * h32).astype(BF)
        y = (-(dtotal * h32 + total * dh32)).astype(BF)
        left = jnp.concatenate([v, z], axis=1)
        stacked = jnp.concatenate([left, jnp.concatenate([u, y], axis=1)], axis=0)
        for early in reversed(range(s)):
            plain, mixed = pair(place(early, s))
            both = mm_nt(stacked, plain)
            gh, dgh = back[early]
            back[early] = [gh + both[:rows], dgh + (both[rows:] + mm_nt(left, mixed))]
        for n, value in enumerate((u, v, z, y)):
            coef[s, 2 + n] = value
        inner = rsum(ga * xa) / width
        dinner = rsum(dga * xa + ga * xd) / width
        total = total + r * r * r * inner
        dtotal = dtotal + r * r * r * dinner - 3.0 * r * r * mu * inner

    me = chip * nc + core
    h, dh, u, v, z, y = [coef[me, n] for n in range(6)]
    for n, value in enumerate((u, y, dh)):
        own_ref[n] = value

    ht, dht, ut, vt, zt, yt = [value.T for value in (h, dh, u, v, z, y)]

    def products(p0, p1, r0t, r1t):
        first = mm(jnp.concatenate([r0t, r1t], axis=1), jnp.concatenate([p0, p1], axis=0))
        return first, mm(r1t, p0)

    for i in range(SECTIONS):
        hi, dhi, ui, vi, zi, yi = [coef[i, n] for n in range(6)]
        below, upto = i < me, i <= me
        m0, m1 = products(
            jnp.where(below, hi, vi),
            jnp.where(below, dhi, ui),
            jnp.where(below, ut, dht),
            jnp.where(below, vt, ht),
        )
        m2, m3 = products(
            jnp.where(upto, hi, zi),
            jnp.where(upto, dhi, yi),
            jnp.where(upto, yt, dht),
            jnp.where(upto, zt, ht),
        )
        keep = i != me
        for n, m in enumerate((jnp.where(keep, m0, 0.0), jnp.where(keep, m1, 0.0), m2, m3)):
            m_ref[i * 4 + n] = m.astype(BF)


def relay(axes, width, pos, ss, parts, g_mine, g_sib):
    rows = ss.shape[0]
    total = 2 * g_mine.shape[0]
    piece = total // (axes[0] * axes[1] * axes[2] * axes[3])
    vm = pl.BlockSpec(memory_space=pltpu.VMEM)
    far = pl.BlockSpec(memory_space=pl.ANY)
    return call(
        functools.partial(relay_kernel, axes, piece, float(width)),
        in_specs=[pl.BlockSpec(memory_space=pltpu.SMEM), vm] + [far] * 10,
        out_specs=[vm, vm],
        out_shape=[
            jax.ShapeDtypeStruct((3, rows, R), BF),
            jax.ShapeDtypeStruct((4 * SECTIONS, R, R), BF),
        ],
        scratch_shapes=[
            pltpu.VMEM((total, R), BF),
            pltpu.VMEM((SECTIONS, rows, 6 * R), BF),
            pltpu.SemaphoreType.DMA,
            pltpu.SemaphoreType.DMA,
            pltpu.VMEM((SECTIONS, 6, rows, R), F32),
            pltpu.VMEM((SECTIONS, 6, rows, R), BF),
        ],
        compiler_params=pltpu.CompilerParams(vmem_limit_bytes=60 * 1024 * 1024),
        cost_estimate=pl.CostEstimate(
            flops=2 * 28 * 12 * rows * R * R, bytes_accessed=total * R * 2, transcendentals=0
        ),
    )(pos, ss, *parts, g_mine, g_sib)


def terms_kernel(pos_ref, x_ref, c_ref, recv_ref, sib_ref, own_ref, far_ref, out_ref):
    first = pos_ref[1] == 0
    part = out_ref.shape[0]
    slab = x_ref.shape[1] // part
    recv, sib = recv_ref[...], sib_ref[...]
    x = jnp.concatenate([x_ref[...], jnp.where(first, recv, sib)], axis=0)
    c = jnp.concatenate([c_ref[...], jnp.where(first, sib, recv)], axis=0)
    u, y, dh = [jnp.concatenate([own_ref[n], far_ref[n]], axis=0) for n in range(3)]
    from_x = mm_tn(x, jnp.concatenate([u, y], axis=1))
    t_in = from_x[:, :R].astype(BF)
    t_out = (from_x[:, R:] + mm_tn(c, dh)).astype(BF)
    for n in range(part):
        out_ref[n, :slab] = t_in[n * slab : (n + 1) * slab]
        out_ref[n, slab : 2 * slab] = t_out[n * slab : (n + 1) * slab]


def terms(pos, slab, room, x, c, recv, recv_sib, own, far):
    rows, width = x.shape
    steps = 4
    block = width // steps
    wide = pl.BlockSpec((rows, block), lambda i: (0, i))
    small = pl.BlockSpec(own.shape, lambda i: (0, 0, 0))
    part = block // slab
    return call(
        terms_kernel,
        grid=(steps,),
        in_specs=[pl.BlockSpec(memory_space=pltpu.SMEM), wide, wide, wide, wide, small, small],
        out_specs=pl.BlockSpec((part, 2 * slab + room, R), lambda i: (i, 0, 0)),
        out_shape=jax.ShapeDtypeStruct((width // slab, 2 * slab + room, R), BF),
        compiler_params=pltpu.CompilerParams(vmem_limit_bytes=14 * 1024 * 1024),
        cost_estimate=pl.CostEstimate(
            flops=4 * rows * width * 3 * R, bytes_accessed=12 * rows * width, transcendentals=0
        ),
    )(pos, x, c, recv, recv_sib, own, far)


def finish_kernel(axes, pos_ref, all_ref, *refs):
    nzh, nc, ny, nx, nzl = axes
    slices, (in_ref, out_ref) = refs[:8], refs[8:]
    chip, core = pos_ref[0], pos_ref[1]
    me = nc * chip + core
    own = slices[0]
    slab = own.shape[1]
    each = 4 * SECTIONS // (ny * nx)
    t = all_ref[0, : 2 * slab].astype(F32)
    for n in range(1, ny * nx):
        t = t + all_ref[n, : 2 * slab].astype(F32)
    t_in, t_out = t[:slab], t[slab:]

    def m_block(at):
        row = 2 * slab + lax.rem(at, each) * R
        return all_ref[at // each, pl.ds(pl.multiple_of(row, 16), R)]

    for n in range(8):
        i = nc * lax.rem(chip + n // 2, nzh) + (core if n % 2 == 0 else 1 - core)
        below = i < me
        a, p, b, q = [slices[n][k] for k in range(4)]
        first = jnp.concatenate([jnp.where(below, b, a), jnp.where(below, q, p)], axis=1)
        ms = [m_block(i * 4 + k) for k in range(4)]
        product = mm_nt(first, jnp.concatenate(ms[:2], axis=1))
        t_in = t_in + jnp.where(below, product, 0.0)
        t_out = t_out + jnp.where(below, 0.0, product)
        t_out = t_out + mm_nt(jnp.concatenate([b, q], axis=1), jnp.concatenate(ms[2:], axis=1))
    in_ref[...] = own[1].astype(F32) * t_in
    out_ref[...] = own[3].astype(F32) * t_out


def finish(axes, pos, arrived, slices):
    vm = pl.BlockSpec(memory_space=pltpu.VMEM)
    shape = jax.ShapeDtypeStruct((slices[0].shape[1], R), F32)
    return call(
        functools.partial(finish_kernel, axes),
        in_specs=[pl.BlockSpec(memory_space=pltpu.SMEM)] + [vm] * 9,
        out_specs=[vm, vm],
        out_shape=[shape, shape],
        compiler_params=pltpu.CompilerParams(vmem_limit_bytes=16 * 1024 * 1024),
    )(pos, arrived, *slices)


def shifted(value, axis, steps):
    count = lax.axis_size(axis)
    return lax.ppermute(value, axis, [(i, (i + steps) % count) for i in range(count)])


def spread(value, axis):
    copies = jnp.broadcast_to(value[None], (lax.axis_size(axis),) + value.shape)
    return lax.all_to_all(copies, axis, 0, 0, tiled=True).reshape((-1,) + value.shape[1:])


def on_device(axes, inputs, cotangent, adapt_in, adapt_out, probe_in, probe_out):
    nzh, nc, ny, nx, nzl = axes
    ndp = ny * nx * nzl
    rows, width = inputs.shape
    slab = width // ndp
    pos = jnp.stack([lax.axis_index(n) for n in SEC + DP]).astype(jnp.int32)
    dp = lax.axis_index(DP)
    sib = lambda w: shifted(w, "c", 1)

    own = jnp.stack(
        [
            lax.dynamic_slice_in_dim(w[0], dp * slab, slab, 0)
            for w in (adapt_in, probe_in, adapt_out, probe_out)
        ]
    )
    prev, after = shifted(own, "zh", 1), shifted(own, "zh", -1)
    own_sib = sib(own)
    projected, ss, keep_x, keep_c, send = project(
        pos, slab, inputs, cotangent, adapt_in, probe_in, adapt_out, probe_out
    )
    prev, after, projected, send = lax.optimization_barrier((prev, after, projected, send))
    prev_sib, after_sib = sib(prev), sib(after)
    partial = gram(pos, own, own_sib, prev, prev_sib, after, after_sib)

    recv = shifted(send, "zl", 1)

    arrived = lax.all_to_all(partial.reshape(ny * nx, -1, R), ("y", "x"), 0, 0, tiled=True)
    arrived, projected = lax.optimization_barrier((arrived, projected))
    near = [projected] + [shifted(projected, "zh", -k) for k in (1, 2, 3)]
    piece = jnp.sum(arrived.astype(F32), axis=0).astype(BF)
    piece = (piece.astype(F32) + shifted(piece, "zl", 1).astype(F32)).astype(BF)
    line = jnp.concatenate([piece] + [shifted(piece, "zh", -k) for k in (1, 2, 3)], axis=0)
    line, recv = lax.optimization_barrier((line, recv))
    g_mine = spread(line, ("y", "x"))
    projected_sib = sib(projected)
    g_mine, near[1:], projected_sib, prev = lax.optimization_barrier(
        (g_mine, near[1:], projected_sib, prev)
    )
    opposite = shifted(prev, "zh", 1)
    parts = [projected, projected_sib] + [v for w in near[1:] for v in (w, sib(w))]
    g_sib = sib(g_mine)

    own3, m_part = relay(axes, width, pos, ss, parts, g_mine, g_sib)
    own3, m_part, opposite = lax.optimization_barrier((own3, m_part, opposite))
    far3 = shifted(own3, "zl", 1)
    m_arrived = lax.all_to_all(m_part.reshape(ny * nx, -1, R), ("y", "x"), 0, 0, tiled=True)
    room = m_arrived.shape[1]
    mine = terms(pos, slab, room, keep_x, keep_c, recv, sib(recv), own3, far3)
    m_arrived, mine = lax.optimization_barrier((m_arrived, mine))
    opposite_sib = sib(opposite)
    m_own = jnp.sum(m_arrived.astype(F32), axis=0)
    m_own = (m_own + shifted(m_own, "zl", 1)).astype(BF)
    copies = jnp.broadcast_to(m_own[None], (ny * nx,) + m_own.shape)
    mine = lax.dynamic_update_slice(mine, copies, (0, 2 * slab, 0))
    mine, opposite_sib = lax.optimization_barrier((mine, opposite_sib))
    arrived = lax.all_to_all(mine, ("y", "x"), 0, 0, tiled=True)
    slices = [own, own_sib, after, after_sib, opposite, opposite_sib, prev, prev_sib]
    diag_in, diag_out = finish(axes, pos, arrived, slices)
    return diag_in[None], diag_out[None]


def solution(mesh, axes=(4, 2, 4, 4, 2)):
    fine = Mesh(mesh.devices.reshape(axes), SEC + DP)
    tokens, weights = P(DP, None), P(SEC, None, None)
    return jax.shard_map(
        functools.partial(on_device, axes),
        mesh=fine,
        in_specs=(tokens, tokens, weights, weights, weights, weights),
        out_specs=(P(SEC, DP, None), P(SEC, DP, None)),
        check_vma=False,
    )
```

```python
import functools

import jax
import jax.numpy as jnp
from jax import lax
from jax.experimental import pallas as pl
from jax.experimental.pallas import tpu as pltpu
from jax.sharding import Mesh, PartitionSpec as P

EPS = 1e-05
R = 128
SECTIONS = 8
BLOCKS = 16
SEC = ("zh", "c")
DP = ("y", "x", "zl")
BF = jnp.bfloat16
F32 = jnp.float32


def mm(left, right):
    return jnp.dot(left, right, preferred_element_type=F32)


def mm_nt(left, right):
    return lax.dot_general(left, right, (((1,), (1,)), ((), ())), preferred_element_type=F32)


def mm_tn(left, right):
    return lax.dot_general(left, right, (((0,), (0,)), ((), ())), preferred_element_type=F32)


def call(kernel, **kw):
    return pl.pallas_call(kernel, **kw)


def project_kernel(slab, pos_ref, x_ref, c_ref, a_ref, p_ref, b_ref, q_ref, *refs):
    out_ref, ss_ref, keep_x_ref, keep_c_ref, send_ref, acc, acc_ss = refs
    step = pl.program_id(0)

    @pl.when(step == 0)
    def _():
        acc[...] = jnp.zeros_like(acc)
        acc_ss[...] = jnp.zeros_like(acc_ss)

    x, c = x_ref[...], c_ref[...]
    rows, width = x.shape
    x32 = x.astype(F32)
    acc_ss[...] += jnp.sum(x32 * x32, axis=-1, keepdims=True)
    ap = jnp.concatenate([a_ref[0], p_ref[0]], axis=1)
    bq = jnp.concatenate([b_ref[0], q_ref[0]], axis=1)
    acc[:, : 2 * R] += mm(x, ap)
    both = mm(jnp.concatenate([x, c], axis=0), bq)
    acc[:, 2 * R : 4 * R] += both[:rows]
    acc[:, 4 * R :] += both[rows:]

    core, odd = pos_ref[1], pos_ref[4] == 1

    def split(value):
        pick = lambda n: jnp.concatenate(
            [value[:, k * slab : (k + 1) * slab] for k in range(n, width // slab, 2)], axis=1
        )
        first, second = pick(0), pick(1)
        return jnp.where(odd, second, first), jnp.where(odd, first, second)

    keep_x, send_x = split(x)
    keep_c, send_c = split(c)
    keep_x_ref[...] = keep_x
    keep_c_ref[...] = keep_c
    send_ref[...] = jnp.where(core == 0, send_x, send_c)

    @pl.when(step == pl.num_programs(0) - 1)
    def _():
        out_ref[...] = acc[...].astype(BF)
        ss_ref[...] = acc_ss[...]


def project(pos, slab, x, c, a, p, b, q):
    rows, width = x.shape
    steps = 4
    block = width // steps
    wide = pl.BlockSpec((rows, block), lambda k: (0, k))
    half = pl.BlockSpec((rows, block // 2), lambda k: (0, k))
    weight = pl.BlockSpec((1, block, R), lambda k: (0, k, 0))
    half_shape = jax.ShapeDtypeStruct((rows, width // 2), BF)
    return call(
        functools.partial(project_kernel, slab),
        grid=(steps,),
        in_specs=[pl.BlockSpec(memory_space=pltpu.SMEM)]
        + [wide, wide, weight, weight, weight, weight],
        out_specs=[
            pl.BlockSpec((rows, 6 * R), lambda k: (0, 0)),
            pl.BlockSpec((rows, R), lambda k: (0, 0)),
            half,
            half,
            half,
        ],
        out_shape=[
            jax.ShapeDtypeStruct((rows, 6 * R), BF),
            jax.ShapeDtypeStruct((rows, R), F32),
            half_shape,
            half_shape,
            half_shape,
        ],
        scratch_shapes=[pltpu.VMEM((rows, 6 * R), F32), pltpu.VMEM((rows, R), F32)],
        compiler_params=pltpu.CompilerParams(vmem_limit_bytes=60 * 1024 * 1024),
        cost_estimate=pl.CostEstimate(
            flops=2 * rows * width * 6 * R,
            bytes_accessed=4 * rows * width + 8 * width * R,
            transcendentals=0,
        ),
    )(pos, x, c, a, p, b, q)


def gram_kernel(pos_ref, own_ref, own_sib_ref, prev_ref, prev_sib_ref, next_ref, next_sib_ref, out_ref):
    chip, core = pos_ref[0], pos_ref[1]

    def cols(value, names):
        return jnp.concatenate([value[n] for n in names], axis=1)

    def four(low, high):
        from_b = mm_tn(low[2], cols(high, (0, 2, 1, 3)))
        from_q = mm_tn(low[3], cols(high, (0, 2)))
        mixed = from_b[:, 2 * R :] + from_q
        return [from_b[:, :R], from_b[:, R : 2 * R], mixed[:, :R], mixed[:, R:]]

    def put(at, block):
        out_ref[at * R : (at + 1) * R] = block.astype(BF)

    own, own_sib = own_ref[...], own_sib_ref[...]
    prev, prev_sib = prev_ref[...], prev_sib_ref[...]
    after, after_sib = next_ref[...], next_sib_ref[...]
    wrap = chip == 3
    for slot, other in enumerate((after, after_sib)):
        pair = four(jnp.where(wrap, other, own), jnp.where(wrap, own, other))
        for i in range(4):
            put(slot * 4 + i, pair[i])
    middle = (chip == 1) | (chip == 2)
    pair = four(jnp.where(middle, prev, after), jnp.where(middle, after, prev_sib))
    for i in range(4):
        put(8 + i, pair[i])
    first = core == 0
    pair = four(jnp.where(first, own, own_sib), jnp.where(first, own_sib, own))
    for i in range(2):
        put(12 + i, jnp.where(first, pair[i], pair[2 + i]))
    self_b = mm_tn(own[2], cols(own, (2, 3)))
    put(14, self_b[:, :R])
    put(15, self_b[:, R:] + mm_tn(own[3], own[2]))


def gram(pos, *slices):
    return call(
        gram_kernel,
        in_specs=[pl.BlockSpec(memory_space=pltpu.SMEM)]
        + [pl.BlockSpec(memory_space=pltpu.VMEM)] * 6,
        out_specs=pl.BlockSpec(memory_space=pltpu.VMEM),
        out_shape=jax.ShapeDtypeStruct((BLOCKS * R, R), BF),
        compiler_params=pltpu.CompilerParams(vmem_limit_bytes=60 * 1024 * 1024),
        cost_estimate=pl.CostEstimate(
            flops=2 * slices[0].shape[1] * BLOCKS * R * R,
            bytes_accessed=slices[0].size * 12,
            transcendentals=0,
        ),
    )(pos, *slices)


def place(low, high):
    gap = high // 2 - low // 2
    same = low % 2 == high % 2
    if gap == 0:
        return [(low, 12), (low, 13), (high, 12), (high, 13)]
    if gap == 2:
        chip = low // 2 + 1 if same else (low // 2 + 3) % 4
        return [(chip * 2 + low % 2, 8 + i) for i in range(4)]
    return [(low if gap == 1 else high, (0 if same else 4) + i) for i in range(4)]


def relay_kernel(axes, piece, width, pos_ref, ss_ref, *refs):
    nzh, nc, ny, nx, nzl = axes
    parts, (g_mine, g_sib, own_ref, m_ref, g, pxc, saved, coef) = refs[:8], refs[8:]
    chip, core = pos_ref[0], pos_ref[1]

    for n in range(8):
        rel, c = n // 2, core if n % 2 == 0 else 1 - core
        section = lax.rem(chip + rel, nzh) * nc + c
        pxc[section] = parts[n][...]
        source = g_mine if n % 2 == 0 else g_sib
        g[section] = source[:, rel]

    def block(at):
        first = at[1] % (piece // R) * R
        return g[at[0], at[1] // (piece // R), first : first + R]

    def pair(at):
        plain = jnp.concatenate([block(at[0]), block(at[1])], axis=1)
        return plain, jnp.concatenate([block(at[2]), block(at[3])], axis=1)

    rows = pxc.shape[1]
    ss = ss_ref[...][:, :1]
    st = jnp.zeros_like(ss)
    rsum = lambda v: jnp.sum(v, axis=-1, keepdims=True)
    hs, dhs, scales, mus = [], [], [], []
    sums = [[pxc[s, :, i * R : (i + 1) * R].astype(F32) for i in range(4)] for s in range(SECTIONS)]
    for s in range(SECTIONS):
        xa, xd, xb, xs = sums[s]
        r = lax.rsqrt(ss / width + EPS)
        mu = r * r * r * (st / width)
        pre = r * xa
        dpre = r * xd - mu * xa
        sig = 1.0 / (1.0 + jnp.exp(-pre))
        slope = sig * (1.0 + pre * (1.0 - sig))
        h = (pre * sig).astype(BF)
        dh = (slope * dpre).astype(BF)
        hs.append(h)
        dhs.append(dh)
        scales.append(r)
        mus.append(mu)
        coef[s, 0] = h
        coef[s, 1] = dh
        stacked = jnp.concatenate([h, dh], axis=0)
        both = mm(stacked, block((s, 14)))
        turn = mm(h, block((s, 15)))
        xb_new = xb + both[:rows]
        xs_new = xs + turn + both[rows:]
        h32, dh32 = h.astype(F32), dh.astype(F32)
        ss = ss + rsum(h32 * (xb + xb_new))
        st = st + rsum(dh32 * xb_new + h32 * (xs + 0.5 * turn))
        for later in range(s + 1, SECTIONS):
            plain, mixed = pair(place(s, later))
            both = mm(stacked, plain)
            cross = mm(h, mixed)
            la, ld, lb, ls = sums[later]
            sums[later] = [
                la + both[:rows, :R],
                ld + (both[rows:, :R] + cross[:, :R]),
                lb + both[:rows, R:],
                ls + (both[rows:, R:] + cross[:, R:]),
            ]
        bend = sig * (1.0 - sig) * (2.0 + pre * (1.0 - 2.0 * sig))
        for i, value in enumerate((xa, xd, xb_new, xs_new, slope, bend * dpre)):
            saved[s, i] = value

    total = jnp.zeros_like(ss)
    dtotal = jnp.zeros_like(ss)
    back = [[pxc[s, :, i * R : (i + 1) * R].astype(F32) for i in (4, 5)] for s in range(SECTIONS)]
    for s in reversed(range(SECTIONS)):
        xa, xd, xb_new, xs_new, slope, curve = [saved[s, i] for i in range(6)]
        gh = back[s][0] - total * xb_new
        dgh = back[s][1] - (dtotal * xb_new + total * xs_new)
        ga = gh * slope
        dga = dgh * slope + gh * curve
        r, mu = scales[s], mus[s]
        u = (r * dga - mu * ga).astype(BF)
        v = (r * ga).astype(BF)
        h32, dh32 = hs[s].astype(F32), dhs[s].astype(F32)
        z = (-total * h32).astype(BF)
        y = (-(dtotal * h32 + total * dh32)).astype(BF)
        left = jnp.concatenate([v, z], axis=1)
        stacked = jnp.concatenate([left, jnp.concatenate([u, y], axis=1)], axis=0)
        for early in reversed(range(s)):
            plain, mixed = pair(place(early, s))
            both = mm_nt(stacked, plain)
            gh, dgh = back[early]
            back[early] = [gh + both[:rows], dgh + (both[rows:] + mm_nt(left, mixed))]
        for n, value in enumerate((u, v, z, y)):
            coef[s, 2 + n] = value
        inner = rsum(ga * xa) / width
        dinner = rsum(dga * xa + ga * xd) / width
        total = total + r * r * r * inner
        dtotal = dtotal + r * r * r * dinner - 3.0 * r * r * mu * inner

    me = chip * nc + core
    h, dh, u, v, z, y = [coef[me, n] for n in range(6)]
    for n, value in enumerate((u, y, dh)):
        own_ref[n] = value

    ht, dht, ut, vt, zt, yt = [value.T for value in (h, dh, u, v, z, y)]

    def products(p0, p1, r0t, r1t):
        first = mm(jnp.concatenate([r0t, r1t], axis=1), jnp.concatenate([p0, p1], axis=0))
        return first, mm(r1t, p0)

    for i in range(SECTIONS):
        hi, dhi, ui, vi, zi, yi = [coef[i, n] for n in range(6)]
        below, upto = i < me, i <= me
        m0, m1 = products(
            jnp.where(below, hi, vi),
            jnp.where(below, dhi, ui),
            jnp.where(below, ut, dht),
            jnp.where(below, vt, ht),
        )
        m2, m3 = products(
            jnp.where(upto, hi, zi),
            jnp.where(upto, dhi, yi),
            jnp.where(upto, yt, dht),
            jnp.where(upto, zt, ht),
        )
        keep = i != me
        for n, m in enumerate((jnp.where(keep, m0, 0.0), jnp.where(keep, m1, 0.0), m2, m3)):
            m_ref[i * 4 + n] = m.astype(BF)


def relay(axes, width, pos, ss, parts, g_mine, g_sib):
    rows = ss.shape[0]
    shape = g_mine.shape
    total = 2 * g_mine.size // R
    vm = pl.BlockSpec(memory_space=pltpu.VMEM)
    return call(
        functools.partial(relay_kernel, axes, shape[2], float(width)),
        in_specs=[pl.BlockSpec(memory_space=pltpu.SMEM)] + [vm] * 11,
        out_specs=[vm, vm],
        out_shape=[
            jax.ShapeDtypeStruct((3, rows, R), BF),
            jax.ShapeDtypeStruct((4 * SECTIONS, R, R), BF),
        ],
        scratch_shapes=[
            pltpu.VMEM((SECTIONS, shape[0]) + shape[2:], BF),
            pltpu.VMEM((SECTIONS, rows, 6 * R), BF),
            pltpu.VMEM((SECTIONS, 6, rows, R), F32),
            pltpu.VMEM((SECTIONS, 6, rows, R), BF),
        ],
        compiler_params=pltpu.CompilerParams(vmem_limit_bytes=32 * 1024 * 1024),
        cost_estimate=pl.CostEstimate(
            flops=2 * 28 * 12 * rows * R * R, bytes_accessed=total * R * 2, transcendentals=0
        ),
    )(pos, ss, *parts, g_mine, g_sib)


def terms_kernel(pos_ref, x_ref, c_ref, recv_ref, sib_ref, own_ref, far_ref, out_ref):
    first = pos_ref[1] == 0
    part = out_ref.shape[0]
    slab = x_ref.shape[1] // part
    recv, sib = recv_ref[...], sib_ref[...]
    x = jnp.concatenate([x_ref[...], jnp.where(first, recv, sib)], axis=0)
    c = jnp.concatenate([c_ref[...], jnp.where(first, sib, recv)], axis=0)
    u, y, dh = [jnp.concatenate([own_ref[n], far_ref[n]], axis=0) for n in range(3)]
    from_x = mm_tn(x, jnp.concatenate([u, y], axis=1))
    t_in = from_x[:, :R].astype(BF)
    t_out = (from_x[:, R:] + mm_tn(c, dh)).astype(BF)
    for n in range(part):
        out_ref[n, :slab] = t_in[n * slab : (n + 1) * slab]
        out_ref[n, slab : 2 * slab] = t_out[n * slab : (n + 1) * slab]


def terms(pos, slab, room, x, c, recv, recv_sib, own, far):
    rows, width = x.shape
    steps = 4
    block = width // steps
    wide = pl.BlockSpec((rows, block), lambda i: (0, i))
    small = pl.BlockSpec(own.shape, lambda i: (0, 0, 0))
    part = block // slab
    return call(
        terms_kernel,
        grid=(steps,),
        in_specs=[pl.BlockSpec(memory_space=pltpu.SMEM), wide, wide, wide, wide, small, small],
        out_specs=pl.BlockSpec((part, 2 * slab + room, R), lambda i: (i, 0, 0)),
        out_shape=jax.ShapeDtypeStruct((width // slab, 2 * slab + room, R), BF),
        compiler_params=pltpu.CompilerParams(vmem_limit_bytes=60 * 1024 * 1024),
        cost_estimate=pl.CostEstimate(
            flops=4 * rows * width * 3 * R, bytes_accessed=12 * rows * width, transcendentals=0
        ),
    )(pos, x, c, recv, recv_sib, own, far)


def finish_kernel(axes, pos_ref, all_ref, *refs):
    nzh, nc, ny, nx, nzl = axes
    slices, (in_ref, out_ref) = refs[:8], refs[8:]
    chip, core = pos_ref[0], pos_ref[1]
    me = nc * chip + core
    own = slices[0]
    slab = own.shape[1]
    each = 4 * SECTIONS // (ny * nx)
    t = all_ref[0, : 2 * slab].astype(F32)
    for n in range(1, ny * nx):
        t = t + all_ref[n, : 2 * slab].astype(F32)
    t_in, t_out = t[:slab], t[slab:]

    def m_block(at):
        row = 2 * slab + lax.rem(at, each) * R
        return all_ref[at // each, pl.ds(pl.multiple_of(row, 16), R)]

    for n in range(8):
        i = nc * lax.rem(chip + n // 2, nzh) + (core if n % 2 == 0 else 1 - core)
        below = i < me
        a, p, b, q = [slices[n][k] for k in range(4)]
        first = jnp.concatenate([jnp.where(below, b, a), jnp.where(below, q, p)], axis=1)
        ms = [m_block(i * 4 + k) for k in range(4)]
        product = mm_nt(first, jnp.concatenate(ms[:2], axis=1))
        t_in = t_in + jnp.where(below, product, 0.0)
        t_out = t_out + jnp.where(below, 0.0, product)
        t_out = t_out + mm_nt(jnp.concatenate([b, q], axis=1), jnp.concatenate(ms[2:], axis=1))
    in_ref[...] = own[1].astype(F32) * t_in
    out_ref[...] = own[3].astype(F32) * t_out


def finish(axes, pos, arrived, slices):
    vm = pl.BlockSpec(memory_space=pltpu.VMEM)
    shape = jax.ShapeDtypeStruct((slices[0].shape[1], R), F32)
    return call(
        functools.partial(finish_kernel, axes),
        in_specs=[pl.BlockSpec(memory_space=pltpu.SMEM)] + [vm] * 9,
        out_specs=[vm, vm],
        out_shape=[shape, shape],
        compiler_params=pltpu.CompilerParams(vmem_limit_bytes=16 * 1024 * 1024),
    )(pos, arrived, *slices)


def shifted(value, axis, steps):
    count = lax.axis_size(axis)
    return lax.ppermute(value, axis, [(i, (i + steps) % count) for i in range(count)])


def spread(value, axis):
    copies = jnp.broadcast_to(value[None], (lax.axis_size(axis),) + value.shape)
    return lax.all_to_all(copies, axis, 0, 0, tiled=True).reshape((-1,) + value.shape[1:])


def on_device(axes, inputs, cotangent, adapt_in, adapt_out, probe_in, probe_out):
    nzh, nc, ny, nx, nzl = axes
    ndp = ny * nx * nzl
    rows, width = inputs.shape
    slab = width // ndp
    pos = jnp.stack([lax.axis_index(n) for n in SEC + DP]).astype(jnp.int32)
    dp = lax.axis_index(DP)
    sib = lambda w: shifted(w, "c", 1)

    own = jnp.stack(
        [
            lax.dynamic_slice_in_dim(w[0], dp * slab, slab, 0)
            for w in (adapt_in, probe_in, adapt_out, probe_out)
        ]
    )
    prev, after = shifted(own, "zh", 1), shifted(own, "zh", -1)
    own_sib = sib(own)
    projected, ss, keep_x, keep_c, send = project(
        pos, slab, inputs, cotangent, adapt_in, probe_in, adapt_out, probe_out
    )
    prev, after, projected, send = lax.optimization_barrier((prev, after, projected, send))
    prev_sib, after_sib = sib(prev), sib(after)
    partial = gram(pos, own, own_sib, prev, prev_sib, after, after_sib)

    recv = shifted(send, "zl", 1)

    arrived = lax.all_to_all(partial.reshape(ny * nx, -1, R), ("y", "x"), 0, 0, tiled=True)
    arrived, projected = lax.optimization_barrier((arrived, projected))
    near = [projected] + [shifted(projected, "zh", -k) for k in (1, 2, 3)]
    piece = jnp.sum(arrived.astype(F32), axis=0).astype(BF)
    piece = (piece.astype(F32) + shifted(piece, "zl", 1).astype(F32)).astype(BF)
    line = jnp.concatenate([piece] + [shifted(piece, "zh", -k) for k in (1, 2, 3)], axis=0)
    line, recv = lax.optimization_barrier((line, recv))
    g_mine = spread(line, ("y", "x"))
    projected_sib = sib(projected)
    g_mine, near[1:], projected_sib, prev = lax.optimization_barrier(
        (g_mine, near[1:], projected_sib, prev)
    )
    opposite = shifted(prev, "zh", 1)
    parts = [projected, projected_sib] + [v for w in near[1:] for v in (w, sib(w))]
    g_sib = sib(g_mine)
    lines = (ny * nx, nzh, -1, R)
    g_mine, g_sib = g_mine.reshape(lines), g_sib.reshape(lines)

    own3, m_part = relay(axes, width, pos, ss, parts, g_mine, g_sib)
    own3, m_part, opposite = lax.optimization_barrier((own3, m_part, opposite))
    far3 = shifted(own3, "zl", 1)
    m_arrived = lax.all_to_all(m_part.reshape(ny * nx, -1, R), ("y", "x"), 0, 0, tiled=True)
    room = m_arrived.shape[1]
    mine = terms(pos, slab, room, keep_x, keep_c, recv, sib(recv), own3, far3)
    m_arrived, mine = lax.optimization_barrier((m_arrived, mine))
    opposite_sib = sib(opposite)
    m_own = jnp.sum(m_arrived.astype(F32), axis=0)
    m_own = (m_own + shifted(m_own, "zl", 1)).astype(BF)
    copies = jnp.broadcast_to(m_own[None], (ny * nx,) + m_own.shape)
    mine = lax.dynamic_update_slice(mine, copies, (0, 2 * slab, 0))
    mine, opposite_sib = lax.optimization_barrier((mine, opposite_sib))
    arrived = lax.all_to_all(mine, ("y", "x"), 0, 0, tiled=True)
    slices = [own, own_sib, after, after_sib, opposite, opposite_sib, prev, prev_sib]
    diag_in, diag_out = finish(axes, pos, arrived, slices)
    return diag_in[None], diag_out[None]


def solution(mesh, axes=(4, 2, 4, 4, 2)):
    fine = Mesh(mesh.devices.reshape(axes), SEC + DP)
    tokens, weights = P(DP, None), P(SEC, None, None)
    return jax.shard_map(
        functools.partial(on_device, axes),
        mesh=fine,
        in_specs=(tokens, tokens, weights, weights, weights, weights),
        out_specs=(P(SEC, DP, None), P(SEC, DP, None)),
        check_vma=False,
    )
```

```python
import functools

import jax
import jax.numpy as jnp
from jax import lax
from jax.experimental import pallas as pl
from jax.experimental.pallas import tpu as pltpu
from jax.sharding import Mesh, PartitionSpec as P

EPS = 1e-05
R = 128
SECTIONS = 8
BLOCKS = 16
SEC = ("zh", "c")
DP = ("y", "x", "zl")
BF = jnp.bfloat16
F32 = jnp.float32


def mm(left, right):
    return jnp.dot(left, right, preferred_element_type=F32)


def mm_nt(left, right):
    return lax.dot_general(left, right, (((1,), (1,)), ((), ())), preferred_element_type=F32)


def mm_tn(left, right):
    return lax.dot_general(left, right, (((0,), (0,)), ((), ())), preferred_element_type=F32)


def call(kernel, **kw):
    return pl.pallas_call(kernel, **kw)


def project_kernel(slab, pos_ref, x_ref, c_ref, a_ref, p_ref, b_ref, q_ref, *refs):
    out_ref, ss_ref, keep_x_ref, keep_c_ref, send_ref, acc, acc_ss = refs
    step = pl.program_id(0)

    @pl.when(step == 0)
    def _():
        acc[...] = jnp.zeros_like(acc)
        acc_ss[...] = jnp.zeros_like(acc_ss)

    x, c = x_ref[...], c_ref[...]
    rows, width = x.shape
    x32 = x.astype(F32)
    acc_ss[...] += jnp.sum(x32 * x32, axis=-1, keepdims=True)
    ap = jnp.concatenate([a_ref[0], p_ref[0]], axis=1)
    bq = jnp.concatenate([b_ref[0], q_ref[0]], axis=1)
    acc[:, : 2 * R] += mm(x, ap)
    both = mm(jnp.concatenate([x, c], axis=0), bq)
    acc[:, 2 * R : 4 * R] += both[:rows]
    acc[:, 4 * R :] += both[rows:]

    core, odd = pos_ref[1], pos_ref[4] == 1

    def split(value):
        pick = lambda n: jnp.concatenate(
            [value[:, k * slab : (k + 1) * slab] for k in range(n, width // slab, 2)], axis=1
        )
        first, second = pick(0), pick(1)
        return jnp.where(odd, second, first), jnp.where(odd, first, second)

    keep_x, send_x = split(x)
    keep_c, send_c = split(c)
    keep_x_ref[...] = keep_x
    keep_c_ref[...] = keep_c
    send_ref[...] = jnp.where(core == 0, send_x, send_c)

    @pl.when(step == pl.num_programs(0) - 1)
    def _():
        out_ref[...] = acc[...].astype(BF)
        ss_ref[...] = acc_ss[...]


def project(pos, slab, x, c, a, p, b, q):
    rows, width = x.shape
    steps = 4
    block = width // steps
    wide = pl.BlockSpec((rows, block), lambda k: (0, k))
    half = pl.BlockSpec((rows, block // 2), lambda k: (0, k))
    weight = pl.BlockSpec((1, block, R), lambda k: (0, k, 0))
    half_shape = jax.ShapeDtypeStruct((rows, width // 2), BF)
    return call(
        functools.partial(project_kernel, slab),
        grid=(steps,),
        in_specs=[pl.BlockSpec(memory_space=pltpu.SMEM)]
        + [wide, wide, weight, weight, weight, weight],
        out_specs=[
            pl.BlockSpec((rows, 6 * R), lambda k: (0, 0)),
            pl.BlockSpec((rows, R), lambda k: (0, 0)),
            half,
            half,
            half,
        ],
        out_shape=[
            jax.ShapeDtypeStruct((rows, 6 * R), BF),
            jax.ShapeDtypeStruct((rows, R), F32),
            half_shape,
            half_shape,
            half_shape,
        ],
        scratch_shapes=[pltpu.VMEM((rows, 6 * R), F32), pltpu.VMEM((rows, R), F32)],
        compiler_params=pltpu.CompilerParams(vmem_limit_bytes=60 * 1024 * 1024),
        cost_estimate=pl.CostEstimate(
            flops=2 * rows * width * 6 * R,
            bytes_accessed=4 * rows * width + 8 * width * R,
            transcendentals=0,
        ),
    )(pos, x, c, a, p, b, q)


def slice_kernel(dp_ref, *refs):
    for n in range(4):
        refs[4][n] = refs[n][0]


def own_slices(dp, slab, *weights):
    block = pl.BlockSpec((1, slab, R), lambda i, dp: (0, dp[0], 0))
    return call(
        slice_kernel,
        grid_spec=pltpu.PrefetchScalarGridSpec(
            num_scalar_prefetch=1,
            grid=(1,),
            in_specs=[block] * 4,
            out_specs=pl.BlockSpec((4, slab, R), lambda i, dp: (0, 0, 0)),
        ),
        out_shape=jax.ShapeDtypeStruct((4, slab, R), BF),
        compiler_params=pltpu.CompilerParams(vmem_limit_bytes=60 * 1024 * 1024),
    )(dp, *weights)


def gram_kernel(pos_ref, own_ref, own_sib_ref, prev_ref, prev_sib_ref, next_ref, next_sib_ref, out_ref):
    chip, core = pos_ref[0], pos_ref[1]

    def cols(value, names):
        return jnp.concatenate([value[n] for n in names], axis=1)

    def four(low, high):
        full = mm_tn(cols(low, (2, 3)), cols(high, (0, 2, 1, 3)))
        from_b, from_q = full[:R], full[R:, : 2 * R]
        mixed = from_b[:, 2 * R :] + from_q
        return [from_b[:, :R], from_b[:, R : 2 * R], mixed[:, :R], mixed[:, R:]]

    def put(at, block):
        out_ref[at * R : (at + 1) * R] = block.astype(BF)

    own, own_sib = own_ref[...], own_sib_ref[...]
    prev, prev_sib = prev_ref[...], prev_sib_ref[...]
    after, after_sib = next_ref[...], next_sib_ref[...]
    wrap = chip == 3
    for slot, other in enumerate((after, after_sib)):
        pair = four(jnp.where(wrap, other, own), jnp.where(wrap, own, other))
        for i in range(4):
            put(slot * 4 + i, pair[i])
    middle = (chip == 1) | (chip == 2)
    pair = four(jnp.where(middle, prev, after), jnp.where(middle, after, prev_sib))
    for i in range(4):
        put(8 + i, pair[i])
    first = core == 0
    pair = four(jnp.where(first, own, own_sib), jnp.where(first, own_sib, own))
    for i in range(2):
        put(12 + i, jnp.where(first, pair[i], pair[2 + i]))
    self_pair = mm_tn(cols(own, (2, 3)), cols(own, (2, 3)))
    put(14, self_pair[:R, :R])
    put(15, self_pair[:R, R:] + self_pair[R:, :R])


def gram(pos, *slices):
    return call(
        gram_kernel,
        in_specs=[pl.BlockSpec(memory_space=pltpu.SMEM)]
        + [pl.BlockSpec(memory_space=pltpu.VMEM)] * 6,
        out_specs=pl.BlockSpec(memory_space=pltpu.VMEM),
        out_shape=jax.ShapeDtypeStruct((BLOCKS * R, R), BF),
        compiler_params=pltpu.CompilerParams(vmem_limit_bytes=60 * 1024 * 1024),
        cost_estimate=pl.CostEstimate(
            flops=2 * slices[0].shape[1] * BLOCKS * R * R,
            bytes_accessed=slices[0].size * 12,
            transcendentals=0,
        ),
    )(pos, *slices)


def place(low, high):
    gap = high // 2 - low // 2
    same = low % 2 == high % 2
    if gap == 0:
        return [(low, 12), (low, 13), (high, 12), (high, 13)]
    if gap == 2:
        chip = low // 2 + 1 if same else (low // 2 + 3) % 4
        return [(chip * 2 + low % 2, 8 + i) for i in range(4)]
    return [(low if gap == 1 else high, (0 if same else 4) + i) for i in range(4)]


def relay_kernel(axes, piece, width, pos_ref, ss_ref, *refs):
    nzh, nc, ny, nx, nzl = axes
    parts, (g_mine, g_sib, own_ref, m_ref, g, pxc, saved, coef) = refs[:8], refs[8:]
    chip, core = pos_ref[0], pos_ref[1]

    for n in range(8):
        rel, c = n // 2, core if n % 2 == 0 else 1 - core
        section = lax.rem(chip + rel, nzh) * nc + c
        pxc[section] = parts[n][...]
        source = g_mine if n % 2 == 0 else g_sib
        g[section] = source[:, rel]

    def block(at):
        first = at[1] % (piece // R) * R
        return g[at[0], at[1] // (piece // R), first : first + R]

    def pair(at):
        plain = jnp.concatenate([block(at[0]), block(at[1])], axis=1)
        return plain, jnp.concatenate([block(at[2]), block(at[3])], axis=1)

    rows = pxc.shape[1]
    ss = ss_ref[...][:, :1]
    st = jnp.zeros_like(ss)
    rsum = lambda v: jnp.sum(v, axis=-1, keepdims=True)
    hs, dhs, scales, mus = [], [], [], []
    sums = [[pxc[s, :, i * R : (i + 1) * R].astype(F32) for i in range(4)] for s in range(SECTIONS)]
    for s in range(SECTIONS):
        xa, xd, xb, xs = sums[s]
        r = lax.rsqrt(ss / width + EPS)
        mu = r * r * r * (st / width)
        pre = r * xa
        dpre = r * xd - mu * xa
        sig = 1.0 / (1.0 + jnp.exp(-pre))
        slope = sig * (1.0 + pre * (1.0 - sig))
        h = (pre * sig).astype(BF)
        dh = (slope * dpre).astype(BF)
        hs.append(h)
        dhs.append(dh)
        scales.append(r)
        mus.append(mu)
        coef[s, 0] = h
        coef[s, 1] = dh
        stacked = jnp.concatenate([h, dh], axis=0)
        both = mm(stacked, block((s, 14)))
        turn = mm(h, block((s, 15)))
        xb_new = xb + both[:rows]
        xs_new = xs + turn + both[rows:]
        h32, dh32 = h.astype(F32), dh.astype(F32)
        ss = ss + rsum(h32 * (xb + xb_new))
        st = st + rsum(dh32 * xb_new + h32 * (xs + 0.5 * turn))
        for later in range(s + 1, SECTIONS):
            plain, mixed = pair(place(s, later))
            both = mm(stacked, plain)
            cross = mm(h, mixed)
            la, ld, lb, ls = sums[later]
            sums[later] = [
                la + both[:rows, :R],
                ld + (both[rows:, :R] + cross[:, :R]),
                lb + both[:rows, R:],
                ls + (both[rows:, R:] + cross[:, R:]),
            ]
        bend = sig * (1.0 - sig) * (2.0 + pre * (1.0 - 2.0 * sig))
        for i, value in enumerate((xa, xd, xb_new, xs_new, slope, bend * dpre)):
            saved[s, i] = value

    total = jnp.zeros_like(ss)
    dtotal = jnp.zeros_like(ss)
    back = [[pxc[s, :, i * R : (i + 1) * R].astype(F32) for i in (4, 5)] for s in range(SECTIONS)]
    for s in reversed(range(SECTIONS)):
        xa, xd, xb_new, xs_new, slope, curve = [saved[s, i] for i in range(6)]
        gh = back[s][0] - total * xb_new
        dgh = back[s][1] - (dtotal * xb_new + total * xs_new)
        ga = gh * slope
        dga = dgh * slope + gh * curve
        r, mu = scales[s], mus[s]
        u = (r * dga - mu * ga).astype(BF)
        v = (r * ga).astype(BF)
        h32, dh32 = hs[s].astype(F32), dhs[s].astype(F32)
        z = (-total * h32).astype(BF)
        y = (-(dtotal * h32 + total * dh32)).astype(BF)
        left = jnp.concatenate([v, z], axis=1)
        stacked = jnp.concatenate([left, jnp.concatenate([u, y], axis=1)], axis=0)
        for early in reversed(range(s)):
            plain, mixed = pair(place(early, s))
            both = mm_nt(stacked, plain)
            gh, dgh = back[early]
            back[early] = [gh + both[:rows], dgh + (both[rows:] + mm_nt(left, mixed))]
        for n, value in enumerate((u, v, z, y)):
            coef[s, 2 + n] = value
        inner = rsum(ga * xa) / width
        dinner = rsum(dga * xa + ga * xd) / width
        total = total + r * r * r * inner
        dtotal = dtotal + r * r * r * dinner - 3.0 * r * r * mu * inner

    me = chip * nc + core
    h, dh, u, v, z, y = [coef[me, n] for n in range(6)]
    for n, value in enumerate((u, y, dh)):
        own_ref[n] = value

    ht, dht, ut, vt, zt, yt = [value.T for value in (h, dh, u, v, z, y)]

    def products(p0, p1, r0t, r1t):
        first = mm(jnp.concatenate([r0t, r1t], axis=1), jnp.concatenate([p0, p1], axis=0))
        return first, mm(r1t, p0)

    for i in range(SECTIONS):
        hi, dhi, ui, vi, zi, yi = [coef[i, n] for n in range(6)]
        below, upto = i < me, i <= me
        m0, m1 = products(
            jnp.where(below, hi, vi),
            jnp.where(below, dhi, ui),
            jnp.where(below, ut, dht),
            jnp.where(below, vt, ht),
        )
        m2, m3 = products(
            jnp.where(upto, hi, zi),
            jnp.where(upto, dhi, yi),
            jnp.where(upto, yt, dht),
            jnp.where(upto, zt, ht),
        )
        keep = i != me
        for n, m in enumerate((jnp.where(keep, m0, 0.0), jnp.where(keep, m1, 0.0), m2, m3)):
            m_ref[i * 4 + n] = m.astype(BF)


def relay(axes, width, pos, ss, parts, g_mine, g_sib):
    rows = ss.shape[0]
    shape = g_mine.shape
    total = 2 * g_mine.size // R
    vm = pl.BlockSpec(memory_space=pltpu.VMEM)
    return call(
        functools.partial(relay_kernel, axes, shape[2], float(width)),
        in_specs=[pl.BlockSpec(memory_space=pltpu.SMEM)] + [vm] * 11,
        out_specs=[vm, vm],
        out_shape=[
            jax.ShapeDtypeStruct((3, rows, R), BF),
            jax.ShapeDtypeStruct((4 * SECTIONS, R, R), BF),
        ],
        scratch_shapes=[
            pltpu.VMEM((SECTIONS, shape[0]) + shape[2:], BF),
            pltpu.VMEM((SECTIONS, rows, 6 * R), BF),
            pltpu.VMEM((SECTIONS, 6, rows, R), F32),
            pltpu.VMEM((SECTIONS, 6, rows, R), BF),
        ],
        compiler_params=pltpu.CompilerParams(vmem_limit_bytes=32 * 1024 * 1024),
        cost_estimate=pl.CostEstimate(
            flops=2 * 28 * 12 * rows * R * R, bytes_accessed=total * R * 2, transcendentals=0
        ),
    )(pos, ss, *parts, g_mine, g_sib)


def terms_kernel(pos_ref, x_ref, c_ref, recv_ref, sib_ref, own_ref, far_ref, out_ref):
    first = pos_ref[1] == 0
    part = out_ref.shape[0]
    slab = x_ref.shape[1] // part
    recv, sib = recv_ref[...], sib_ref[...]
    x = jnp.concatenate([x_ref[...], jnp.where(first, recv, sib)], axis=0)
    c = jnp.concatenate([c_ref[...], jnp.where(first, sib, recv)], axis=0)
    u, y, dh = [jnp.concatenate([own_ref[n], far_ref[n]], axis=0) for n in range(3)]
    from_x = mm_tn(x, jnp.concatenate([u, y], axis=1))
    t_in = from_x[:, :R].astype(BF)
    t_out = (from_x[:, R:] + mm_tn(c, dh)).astype(BF)
    for n in range(part):
        out_ref[n, :slab] = t_in[n * slab : (n + 1) * slab]
        out_ref[n, slab : 2 * slab] = t_out[n * slab : (n + 1) * slab]


def terms(pos, slab, room, x, c, recv, recv_sib, own, far):
    rows, width = x.shape
    steps = 4
    block = width // steps
    wide = pl.BlockSpec((rows, block), lambda i: (0, i))
    small = pl.BlockSpec(own.shape, lambda i: (0, 0, 0))
    part = block // slab
    return call(
        terms_kernel,
        grid=(steps,),
        in_specs=[pl.BlockSpec(memory_space=pltpu.SMEM), wide, wide, wide, wide, small, small],
        out_specs=pl.BlockSpec((part, 2 * slab + room, R), lambda i: (i, 0, 0)),
        out_shape=jax.ShapeDtypeStruct((width // slab, 2 * slab + room, R), BF),
        compiler_params=pltpu.CompilerParams(vmem_limit_bytes=60 * 1024 * 1024),
        cost_estimate=pl.CostEstimate(
            flops=4 * rows * width * 3 * R, bytes_accessed=12 * rows * width, transcendentals=0
        ),
    )(pos, x, c, recv, recv_sib, own, far)


def finish_kernel(axes, pos_ref, all_ref, *refs):
    nzh, nc, ny, nx, nzl = axes
    slices, (in_ref, out_ref) = refs[:8], refs[8:]
    chip, core = pos_ref[0], pos_ref[1]
    me = nc * chip + core
    own = slices[0]
    slab = own.shape[1]
    each = 4 * SECTIONS // (ny * nx)
    t = all_ref[0, : 2 * slab].astype(F32)
    for n in range(1, ny * nx):
        t = t + all_ref[n, : 2 * slab].astype(F32)
    t_in, t_out = t[:slab], t[slab:]

    def m_block(at):
        row = 2 * slab + lax.rem(at, each) * R
        return all_ref[at // each, pl.ds(pl.multiple_of(row, 16), R)]

    for n in range(8):
        i = nc * lax.rem(chip + n // 2, nzh) + (core if n % 2 == 0 else 1 - core)
        below = i < me
        a, p, b, q = [slices[n][k] for k in range(4)]
        first = jnp.concatenate([jnp.where(below, b, a), jnp.where(below, q, p)], axis=1)
        ms = [m_block(i * 4 + k) for k in range(4)]
        product = mm_nt(first, jnp.concatenate(ms[:2], axis=1))
        t_in = t_in + jnp.where(below, product, 0.0)
        t_out = t_out + jnp.where(below, 0.0, product)
        t_out = t_out + mm_nt(jnp.concatenate([b, q], axis=1), jnp.concatenate(ms[2:], axis=1))
    in_ref[...] = own[1].astype(F32) * t_in
    out_ref[...] = own[3].astype(F32) * t_out


def finish(axes, pos, arrived, slices):
    vm = pl.BlockSpec(memory_space=pltpu.VMEM)
    shape = jax.ShapeDtypeStruct((slices[0].shape[1], R), F32)
    return call(
        functools.partial(finish_kernel, axes),
        in_specs=[pl.BlockSpec(memory_space=pltpu.SMEM)] + [vm] * 9,
        out_specs=[vm, vm],
        out_shape=[shape, shape],
        compiler_params=pltpu.CompilerParams(vmem_limit_bytes=16 * 1024 * 1024),
    )(pos, arrived, *slices)


def shifted(value, axis, steps):
    count = lax.axis_size(axis)
    return lax.ppermute(value, axis, [(i, (i + steps) % count) for i in range(count)])


def spread(value, axis):
    copies = jnp.broadcast_to(value[None], (lax.axis_size(axis),) + value.shape)
    return lax.all_to_all(copies, axis, 0, 0, tiled=True).reshape((-1,) + value.shape[1:])


def on_device(axes, inputs, cotangent, adapt_in, adapt_out, probe_in, probe_out):
    nzh, nc, ny, nx, nzl = axes
    ndp = ny * nx * nzl
    rows, width = inputs.shape
    slab = width // ndp
    pos = jnp.stack([lax.axis_index(n) for n in SEC + DP]).astype(jnp.int32)
    dp = lax.axis_index(DP)
    sib = lambda w: shifted(w, "c", 1)

    own = own_slices(dp.astype(jnp.int32).reshape(1), slab, adapt_in, probe_in, adapt_out, probe_out)
    prev, after = shifted(own, "zh", 1), shifted(own, "zh", -1)
    own_sib = sib(own)
    projected, ss, keep_x, keep_c, send = project(
        pos, slab, inputs, cotangent, adapt_in, probe_in, adapt_out, probe_out
    )
    prev, after, projected, send = lax.optimization_barrier((prev, after, projected, send))
    prev_sib, after_sib = sib(prev), sib(after)
    partial = gram(pos, own, own_sib, prev, prev_sib, after, after_sib)

    recv = shifted(send, "zl", 1)

    arrived = lax.all_to_all(partial.reshape(ny * nx, -1, R), ("y", "x"), 0, 0, tiled=True)
    arrived, projected = lax.optimization_barrier((arrived, projected))
    near = [projected] + [shifted(projected, "zh", -k) for k in (1, 2, 3)]
    piece = jnp.sum(arrived.astype(F32), axis=0).astype(BF)
    piece = (piece.astype(F32) + shifted(piece, "zl", 1).astype(F32)).astype(BF)
    line = jnp.concatenate([piece] + [shifted(piece, "zh", -k) for k in (1, 2, 3)], axis=0)
    line, recv = lax.optimization_barrier((line, recv))
    g_mine = spread(line, ("y", "x"))
    projected_sib = sib(projected)
    g_mine, near[1:], projected_sib, prev = lax.optimization_barrier(
        (g_mine, near[1:], projected_sib, prev)
    )
    opposite = shifted(prev, "zh", 1)
    parts = [projected, projected_sib] + [v for w in near[1:] for v in (w, sib(w))]
    g_sib = sib(g_mine)
    lines = (ny * nx, nzh, -1, R)
    g_mine, g_sib = g_mine.reshape(lines), g_sib.reshape(lines)

    own3, m_part = relay(axes, width, pos, ss, parts, g_mine, g_sib)
    own3, m_part, opposite = lax.optimization_barrier((own3, m_part, opposite))
    far3 = shifted(own3, "zl", 1)
    m_arrived = lax.all_to_all(m_part.reshape(ny * nx, -1, R), ("y", "x"), 0, 0, tiled=True)
    room = m_arrived.shape[1]
    mine = terms(pos, slab, room, keep_x, keep_c, recv, sib(recv), own3, far3)
    m_arrived, mine = lax.optimization_barrier((m_arrived, mine))
    opposite_sib = sib(opposite)
    m_own = jnp.sum(m_arrived.astype(F32), axis=0)
    m_own = (m_own + shifted(m_own, "zl", 1)).astype(BF)
    copies = jnp.broadcast_to(m_own[None], (ny * nx,) + m_own.shape)
    mine = lax.dynamic_update_slice(mine, copies, (0, 2 * slab, 0))
    mine, opposite_sib = lax.optimization_barrier((mine, opposite_sib))
    arrived = lax.all_to_all(mine, ("y", "x"), 0, 0, tiled=True)
    slices = [own, own_sib, after, after_sib, opposite, opposite_sib, prev, prev_sib]
    diag_in, diag_out = finish(axes, pos, arrived, slices)
    return diag_in[None], diag_out[None]


def solution(mesh, axes=(4, 2, 4, 4, 2)):
    fine = Mesh(mesh.devices.reshape(axes), SEC + DP)
    tokens, weights = P(DP, None), P(SEC, None, None)
    return jax.shard_map(
        functools.partial(on_device, axes),
        mesh=fine,
        in_specs=(tokens, tokens, weights, weights, weights, weights),
        out_specs=(P(SEC, DP, None), P(SEC, DP, None)),
        check_vma=False,
    )
```
